256 devices in a mesh: sec: 2 (over core), tile: 32 (over y, z), harm: 4 (over x).
Axes of the slice: x: 4, y: 4, z: 8, core: 2. Of those that a mesh axis runs over, the one named last changes fastest.
Arguments:
- state: float32 [2, 3, 16, 8192, 256], P('sec', None, 'harm', 'tile'), may hold values from -6 to 6
- forcing: float32 [2, 2, 16, 8192, 256], P('sec', None, 'harm', 'tile'), may hold values from -6 to 6
- depth: float32 [2, 8192, 256], P('sec', 'tile'), may hold values from 0.2 to 2
- wet_mask: int32 [2, 8192, 256], P('sec', 'tile'), may hold values 0 or 1
- nest_index: int32 [8192], P('tile'), may hold values from 0 to 65535
- freq_order: int32 [16], replicated, may hold values from 0 to 15, each once
Outputs:
- new_state: float32 [2, 3, 16, 8192, 256], P('sec', None, 'harm', 'tile')
The draws below stay inside these ranges and needn't reach their ends.
Inputs may be any that keep to these rules, and one draw needn't show every extreme that they name: `freq_order`: each index of the frequency table appears once.
All inputs are finite; a program needn't handle non-finite values. No bound on the sum of `wet_mask` on one device may be relied on, other than what follows from the above.
Results may differ from the reference program's by a relative error of at most 0.00011.
Values sent between devices are 32-bit elements; how exact they have to be, the bound alone decides.
No kernel may reach another device: no remote copies, remote signals or barrier semaphores. Data moves between devices by JAX's collectives and lax.ppermute only.
A program may use at most 320 MiB of HBM per device.

```python
import math
import jax
import jax.numpy as jnp
from jax import lax

K = 8
H = 16
NT = 64
NFREQ = 16
CR = 256
CC = 256
ROWS = 8192
N_SEC = 2
N_TILE = 32


def set_ends(values, key, least, high):
    shape = values.shape
    index_at = [jax.random.randint(jax.random.fold_in(key, axis), (), 0, shape[axis]) for axis in range(len(shape))]
    values = values.at[tuple(index_at)].set(least)
    longest = shape.index(max(shape))
    index_at[longest] = (index_at[longest] + 1) % shape[longest]
    return values.at[tuple(index_at)].set(high)


def shard_levels(stream_key, extent, cuts, low, top_value):
    factor_of = 1.0
    for axis_at, shards_of in cuts:
        draws = jax.random.uniform(jax.random.fold_in(jax.random.fold_in(stream_key, 6), axis_at), (shards_of,), jnp.float32, low / len(cuts), top_value / len(cuts))
        factor_of = factor_of * jnp.repeat(jnp.exp(draws), extent[axis_at] // shards_of).reshape((-1,) + (1,) * (len(extent) - 1 - axis_at))
    return factor_of


def centred(rng, dims, scale, reach, pieces=(), dtype=jnp.bfloat16):
    drawn = jax.random.normal(rng, dims, jnp.float32) * scale
    if len(pieces) > 0:
        drawn = shard_levels(rng, dims, pieces, -0.22, 0.18) * drawn
    return jnp.clip(drawn, min=-reach, max=reach).astype(dtype)


def setup_inputs(seed: int = 0) -> dict:
    arg_keys = jax.random.split(jax.random.key(seed), 7)
    state = centred(arg_keys[0], (N_SEC, 3, H, ROWS, CC), 1.0, 6.0, ((0, 2), (2, 4), (3, 32)), jnp.float32)
    forcing = centred(arg_keys[1], (N_SEC, 2, H, ROWS, CC), 1.0, 6.0, ((0, 2), (2, 4), (3, 32)), jnp.float32)
    depth = jnp.clip(jnp.exp(math.log(2.0) - 2.3025851 * jax.random.uniform(arg_keys[2], (N_SEC, ROWS, CC), jnp.float32) ** shard_levels(arg_keys[2], (N_SEC, ROWS, CC), ((0, 2), (1, 32)), -0.2, 0.2)), 0.2, 2.0)
    wet_mask = set_ends((jax.random.randint(arg_keys[3], (N_SEC, ROWS, CC), 0, 4) < 3).astype(jnp.int32), jax.random.fold_in(arg_keys[3], 1), 0, 1)
    nest_index = set_ends(jax.random.randint(arg_keys[4], (N_TILE * CR,), 0, CR * CC), jax.random.fold_in(arg_keys[4], 1), 0, (CR * CC) - 1).astype(jnp.int32)
    freq_order = jax.random.permutation(arg_keys[5], NFREQ).astype(jnp.int32)
    return dict(state=state, forcing=forcing, depth=depth, wet_mask=wet_mask, nest_index=nest_index, freq_order=freq_order)


gravity = 1.0
relax_step = 0.3
drag_coef = 0.5
speed_floor = 0.01
omega_step = 0.1

def make_basis(freq_order):
    cycles = (freq_order[:K] + 1).astype(jnp.float32)
    samples = jnp.arange(NT).astype(jnp.float32)
    angle = 2.0 * math.pi / NT * samples[:, None] * cycles[None, :]
    basis = jnp.stack([jnp.cos(angle), jnp.sin(angle)], axis=-1).reshape(NT, H)
    return (basis, omega_step * cycles)

def friction_terms(coeffs, basis):
    samples = jnp.einsum('th,fahn->fatn', basis, coeffs, precision=lax.Precision.HIGHEST)
    speed = jnp.sqrt(samples[0] * samples[0] + samples[1] * samples[1] + speed_floor)
    return 2.0 / NT * jnp.einsum('th,fatn->fahn', basis, speed[None] * samples, precision=lax.Precision.HIGHEST)

def rotate(field, omega):
    pairs = field.reshape((omega.shape[0], 2) + field.shape[1:])
    scale = omega[:, None, None]
    return jnp.stack([scale * pairs[:, 1], -scale * pairs[:, 0]], axis=1).reshape(field.shape)

def diff_cols(field):
    padded = jnp.pad(field, ((0, 0), (0, 0), (1, 1)))
    return 0.5 * (padded[:, :, 2:] - padded[:, :, :-2])

def diff_rows(field):
    padded = jnp.pad(field, ((0, 0), (1, 1), (0, 0)))
    return 0.5 * (padded[:, 2:] - padded[:, :-2])

def reference(state, forcing, depth, wet_mask, nest_index, freq_order):
    basis, omega = make_basis(freq_order)
    global_cells = state[0].reshape(3, H, N_TILE, CR * CC)
    index_table = nest_index.reshape(N_TILE, CR).astype(jnp.int32)
    strip = jnp.take_along_axis(global_cells, index_table[None, None], axis=3).reshape(3, H, ROWS)
    outputs = []
    for section in range(2):
        fields = state[section]
        if section == 1:
            fields = fields.at[:, :, :, 0].set(strip)
        eta, east, north = (fields[0], fields[1], fields[2])
        wet = wet_mask[section].astype(jnp.float32)
        height = depth[section]
        coupled = jnp.stack([east, north]).reshape(2, H, N_TILE, CR * CC)
        coupled = jnp.moveaxis(coupled, 2, 0)

        def per_tile(block):
            return friction_terms(block[:, None], basis)[:, 0]
        friction = lax.map(per_tile, coupled)
        friction = jnp.moveaxis(friction, 0, 2).reshape(2, H, ROWS, CC)
        friction = friction * (drag_coef / height)[None, None]
        res_east = rotate(east, omega) + gravity * diff_cols(eta) + friction[0] - forcing[section, 0]
        res_north = rotate(north, omega) + gravity * diff_rows(eta) + friction[1] - forcing[section, 1]
        east_new = wet * (east - relax_step * res_east)
        north_new = wet * (north - relax_step * res_north)
        res_eta = rotate(eta, omega) + diff_cols(height * east_new) + diff_rows(height * north_new)
        eta_new = wet * (eta - relax_step * res_eta)
        outputs.append(jnp.stack([eta_new, east_new, north_new]))
    return jnp.stack(outputs)
```

```python
import functools

import jax
import jax.numpy as jnp
from jax import lax
from jax.experimental import pallas as pl
from jax.experimental.pallas import tpu as pltpu
from jax.sharding import PartitionSpec as P

K = 8
NT = 64
CELLS = 256
RING = 4
HALF = 128
PIECE = 32
LANES = 128
BLOCK = 8 * PIECE
relax_step = 0.3
speed_floor = 0.01
omega_step = 0.1
TURN = 6.283185307179586 / NT
F32 = jnp.float32
BF16 = jnp.bfloat16
I32 = jnp.int32
MIB = 1 << 20


def params(mib=48):
    return pltpu.CompilerParams(vmem_limit_bytes=mib * MIB)


def cost(us):
    return pl.CostEstimate(flops=0, bytes_accessed=int(us * 3.0e6), transcendentals=0)


def vmem(count):
    return [pl.BlockSpec(memory_space=pltpu.VMEM)] * count


def dot(a, b):
    return jnp.dot(a, b, preferred_element_type=F32)


def pair(x):
    high = x.astype(BF16)
    return high, (x - high.astype(F32)).astype(BF16)


def iota(shape, dim):
    return lax.broadcasted_iota(I32, shape, dim)


def trig(freq_ref, me, time, slot, channel):
    owner = (me - slot + RING) & (RING - 1)
    constituent = owner * 2 + (channel >> 1)
    cycles = jnp.zeros(time.shape, I32)
    for k in range(K):
        cycles = jnp.where(constituent == k, freq_ref[k] + 1, cycles)
    angle = ((time * cycles) & (NT - 1)).astype(F32) * TURN
    return jnp.where((channel & 1) == 0, jnp.cos(angle), jnp.sin(angle))


def prepare(freq_ref, index_ref, fields_ref, strip_ref, forward_ref, backward_ref):
    me = lax.axis_index("harm")
    index = index_ref[...]
    row_of, col_of = index >> 8, index & (CELLS - 1)
    pick = jnp.where(iota((CELLS, CELLS), 0) == col_of, 1.0, 0.0).astype(BF16)
    picks = jnp.concatenate([pick, pick, pick], 0)
    at_row = iota((CELLS, CELLS), 0) == row_of
    for k in range(12):
        plane = fields_ref[k]
        high, rest = plane.astype(BF16), None
        rest = plane - high.astype(F32)
        mid, low = pair(rest)
        column = dot(jnp.concatenate([high, mid, low], 1), picks)
        strip_ref[k : k + 1, :] = jnp.sum(jnp.where(at_row, column, 0.0), axis=0, keepdims=True)
    shape = (128, 96)
    row, col = iota(shape, 0), iota(shape, 1)
    part, lane = col >> 5, col & 31
    value = trig(freq_ref, me, row & 63, lane >> 3, lane & 3)
    value = jnp.where((row >> 6) == ((lane >> 2) & 1), value, 0.0)
    high = value.astype(BF16).astype(F32)
    forward_ref[...] = jnp.where(part == 1, value - high, high).astype(BF16)
    shape = (64, 256)
    row, col = iota(shape, 0), iota(shape, 1)
    lane = row & 31
    value = trig(freq_ref, me, col & 63, lane >> 3, lane & 3) * (1.0 / NT)
    value = jnp.where(((col >> 6) & 1) == ((lane >> 2) & 1), value, 0.0)
    high = value.astype(BF16).astype(F32)
    low = jnp.where(col < 128, value - high, 0.0)
    backward_ref[...] = jnp.where(row < 32, high, low).astype(BF16)


def pieces(state_ref, outs, sems, start):
    me = lax.axis_index("harm")
    copies = []
    for slot in range(RING):
        row = pl.multiple_of(start + ((me + slot) & (RING - 1)) * PIECE, PIECE)
        for j in range(2):
            copies.append(
                pltpu.make_async_copy(
                    state_ref.at[0, pl.ds(1, 2), :, pl.ds(row, PIECE), pl.ds(j * LANES, LANES)],
                    outs[slot].at[pl.ds(j * BLOCK, BLOCK), :].reshape(2, 4, PIECE, LANES),
                    sems.at[slot, j],
                )
            )
    for copy in copies:
        copy.start()
    return copies


def pack_upper(state_ref, *refs):
    for copy in pieces(state_ref, refs[:4], refs[4], 0):
        copy.wait()


def pack_lower(strip_ref, state_ref, *refs):
    outs, (first_ref, last_ref, edges, sems, edge_sems) = refs[:4], refs[4:]
    shelf = lax.axis_index("sec") == 1
    looks = [
        pltpu.make_async_copy(state_ref.at[0, :, :, pl.ds(row, 8), :], edges.at[e], edge_sems.at[e])
        for e, row in enumerate((0, CELLS - 8))
    ]
    for look in looks:
        look.start()
    copies = pieces(state_ref, outs, sems, HALF)
    for look in looks:
        look.wait()
    strip = strip_ref[...]
    take = jnp.logical_and(iota((12, CELLS), 1) == 0, shelf)
    first = edges[0].reshape(12, 8, CELLS)[:, 0, :]
    last = edges[1].reshape(12, 8, CELLS)[:, 7, :]
    first = jnp.where(take, strip[:, 0:1], first)
    last = jnp.where(take, strip[:, CELLS - 1 : CELLS], last)
    first_ref[...] = first[0:4]
    last_ref[...] = last[0:4]
    for e, values in enumerate((strip, first, last)):
        for j in range(2):
            row = 2 * BLOCK + 24 * j + 8 * e
            for slot in range(RING):
                outs[slot][row : row + 8, :] = values[4:12, j * LANES : (j + 1) * LANES]
    for copy in copies:
        copy.wait()


def friction(more, forward_ref, backward_ref, *refs):
    xs, outs = refs[:RING], refs[RING : 2 * RING]
    forward, backward = forward_ref[...], backward_ref[...]

    def terms(x):
        high, low = pair(x)
        samples = dot(forward, jnp.concatenate([high, high, low], 0))
        east, north = samples[:NT], samples[NT:]
        square = east * east + north * north + speed_floor
        speed = square * lax.rsqrt(square)
        high, low = pair(jnp.concatenate([speed * east, speed * north], 0))
        both = dot(backward, jnp.concatenate([high, low], 0))
        return both[:32] + both[32:]

    def step(r, carry):
        x = jnp.concatenate(
            [
                jnp.concatenate([ref[pl.ds(j * BLOCK + r, 8, stride=PIECE), :] for ref in xs], 0)
                for j in range(2)
            ],
            1,
        )
        out = terms(x)
        for slot in range(RING):
            for j in range(2):
                outs[slot][pl.ds(j * BLOCK + r, 8, stride=PIECE), :] = out[
                    8 * slot : 8 * slot + 8, j * LANES : (j + 1) * LANES
                ]
        return carry

    lax.fori_loop(0, PIECE, step, 0, unroll=4)
    if more:
        for e in range(3):
            rows = [pl.ds(2 * BLOCK + 24 * j + 8 * e, 8) for j in range(2)]
            x = jnp.concatenate(
                [jnp.concatenate([ref[rows[j], :] for ref in xs], 0) for j in range(2)], 1
            )
            refs[2 * RING][8 * e : 8 * e + 8, :] = terms(x)[:8]


def left_right(x):
    lane = iota(x.shape, 1)
    right = jnp.where(lane == CELLS - 1, 0.0, pltpu.roll(x, CELLS - 1, 1))
    left = jnp.where(lane == 0, 0.0, pltpu.roll(x, 1, 1))
    return right - left


def up_down(x, before, after):
    row = iota(x.shape, 0)
    down = jnp.where(row == CELLS - 1, after, pltpu.roll(x, CELLS - 1, 0))
    up = jnp.where(row == 0, before, pltpu.roll(x, 1, 0))
    return down - up


def known(freq_ref, strip_ref, before_ref, after_ref, state_ref, forcing_ref, east_ref, north_ref, eta_ref, edge_ref):
    me = lax.axis_index("harm")
    shelf = lax.axis_index("sec") == 1
    take = jnp.logical_and(iota((CELLS, CELLS), 1) == 0, shelf)
    columns = jnp.concatenate([strip_ref[...], jnp.zeros((4, CELLS), F32)], 0).T

    def field(f, ch):
        k = 4 * f + ch
        return jnp.where(take, columns[:, k : k + 1], state_ref[0, f, ch])

    for i in range(2):
        omega = omega_step * (freq_ref[2 * me + i] + 1).astype(F32)
        eta = [field(0, 2 * i + p) for p in range(2)]
        for p in range(2):
            ch = 2 * i + p
            turn = -omega if p else omega
            eta_ref[ch] = eta[p] - relax_step * (turn * eta[1 - p])
        east = [field(1, 2 * i + p) for p in range(2)]
        for p in range(2):
            ch = 2 * i + p
            turn = -omega if p else omega
            rest = turn * east[1 - p] + 0.5 * left_right(eta[p]) - forcing_ref[0, 0, ch]
            east_ref[ch] = east[p] - relax_step * rest
        north = [field(2, 2 * i + p) for p in range(2)]
        for p in range(2):
            ch = 2 * i + p
            turn = -omega if p else omega
            slope = up_down(eta[p], before_ref[ch : ch + 1, :], after_ref[ch : ch + 1, :])
            rest = turn * north[1 - p] + 0.5 * slope - forcing_ref[0, 1, ch]
            value = north[p] - relax_step * rest
            north_ref[ch] = value
            edge_ref[ch : ch + 1, :] = value[0:1, :]
            edge_ref[4 + ch : 5 + ch, :] = value[CELLS - 1 : CELLS, :]


def edge_flux(edge_ref, extra_ref, depth_ref, wet_ref, first_ref, last_ref):
    for out_ref, at, row in ((first_ref, 0, 0), (last_ref, 1, CELLS - 1)):
        height = depth_ref[0, row : row + 1, :]
        wet = wet_ref[0, row : row + 1, :].astype(F32)
        drag = extra_ref[8 + 8 * at + 4 : 8 + 8 * at + 8, :]
        north = wet * (edge_ref[4 * at : 4 * at + 4, :] - (relax_step / height) * drag)
        out_ref[...] = height * north


def finish(extra_ref, before_ref, after_ref, depth_ref, wet_ref, east_ref, north_ref, eta_ref, *refs):
    drags, out_ref = refs[:-1], refs[-1]
    me = lax.axis_index("harm")
    shelf = lax.axis_index("sec") == 1
    columns = extra_ref[0:8, :].T
    for c in range(2):
        for slot in range(RING):
            row = pl.multiple_of(c * HALF + ((me + slot) & (RING - 1)) * PIECE, PIECE)
            rows = pl.ds(row, PIECE)
            wet = wet_ref[0, rows, :].astype(F32)
            factor = relax_step / depth_ref[0, rows, :]
            drag_ref = drags[4 * c + slot]
            for k in range(8):
                drag = jnp.concatenate(
                    [drag_ref[pl.ds(j * BLOCK + k * PIECE, PIECE), :] for j in range(2)], 1
                )
                source = (east_ref, north_ref)[k // 4]
                out_ref[0, 1 + k // 4, k % 4, rows, :] = wet * (source[k % 4, rows, :] - factor * drag)
    height = depth_ref[0]
    wet = wet_ref[0].astype(F32)
    factor = relax_step / height
    first = jnp.logical_and(iota((CELLS, CELLS), 1) == 0, shelf)
    for k in range(8):
        source = (east_ref, north_ref)[k // 4]
        fixed = wet * (source[k % 4] - factor * columns[:, k : k + 1])
        lanes = pl.ds(0, 128)
        out_ref[0, 1 + k // 4, k % 4, :, lanes] = jnp.where(
            first[:, :128], fixed[:, :128], out_ref[0, 1 + k // 4, k % 4, :, lanes]
        )
    for ch in range(4):
        slope = left_right(height * out_ref[0, 1, ch])
        slope = slope + up_down(
            height * out_ref[0, 2, ch], before_ref[ch : ch + 1, :], after_ref[ch : ch + 1, :]
        )
        out_ref[0, 0, ch] = wet * (eta_ref[ch] - (0.5 * relax_step) * slope)


def around(value, steps):
    return lax.ppermute(value, "harm", [(i, (i + steps) % RING) for i in range(RING)])


def body(state, forcing, depth, wet_mask, nest_index, freq_order):
    me = lax.axis_index("harm")
    tiles = lax.axis_size("tile")
    smem = pl.BlockSpec(memory_space=pltpu.SMEM)
    hbm = pl.BlockSpec(memory_space=pl.ANY)
    array = jax.ShapeDtypeStruct

    half = array((2 * BLOCK, LANES), F32)
    parts = pl.pallas_call(
        pack_upper,
        name="pack_upper",
        in_specs=[hbm],
        out_specs=vmem(RING),
        out_shape=(half,) * RING,
        scratch_shapes=[pltpu.SemaphoreType.DMA((RING, 2))],
        compiler_params=params(),
        cost_estimate=cost(2),
    )(state)
    upper = [parts[0]] + [around(parts[slot], slot) for slot in (1, 2, 3)]

    strip, forward, backward = pl.pallas_call(
        prepare,
        name="prepare",
        in_specs=[smem] + vmem(2),
        out_specs=vmem(3),
        out_shape=(array((12, CELLS), F32), array((128, 96), BF16), array((64, 256), BF16)),
        compiler_params=params(),
        cost_estimate=cost(4),
    )(freq_order, nest_index.reshape(1, CELLS), state.reshape(12, CELLS, CELLS))
    strip = lax.ppermute(strip, "sec", [(0, 1)])

    packed = pl.pallas_call(
        pack_lower,
        name="pack_lower",
        in_specs=vmem(1) + [hbm],
        out_specs=vmem(6),
        out_shape=(array((2 * BLOCK + 48, LANES), F32),) * RING + (array((4, CELLS), F32),) * 2,
        scratch_shapes=[
            pltpu.VMEM((2, 3, 4, 8, CELLS), F32),
            pltpu.SemaphoreType.DMA((RING, 2)),
            pltpu.SemaphoreType.DMA((2,)),
        ],
        compiler_params=params(),
        cost_estimate=cost(2),
    )(strip, state)
    lower = [packed[0]] + [around(packed[slot], slot) for slot in (1, 2, 3)]
    to_next = [(i, i + 1) for i in range(tiles - 1)]
    to_last = [(i + 1, i) for i in range(tiles - 1)]
    after = lax.ppermute(packed[4], "tile", to_last)
    before = lax.ppermute(packed[5], "tile", to_next)

    def drag(xs, more):
        outs = (half,) * RING + (array((24, CELLS), F32),) * more
        return pl.pallas_call(
            functools.partial(friction, more),
            name="friction",
            in_specs=vmem(2 + RING),
            out_specs=vmem(len(outs)),
            out_shape=outs,
            compiler_params=params(),
            cost_estimate=cost(10),
        )(forward, backward, *xs)

    upper_terms = drag(upper, 0)
    upper_back = [upper_terms[0]] + [around(upper_terms[slot], -slot) for slot in (1, 2, 3)]
    lower_terms = drag(lower, 1)
    lower_back = [lower_terms[0]] + [around(lower_terms[slot], -slot) for slot in (1, 2, 3)]
    extra = lower_terms[RING]

    plane = array((4, CELLS, CELLS), F32)
    east, north, eta, edge = pl.pallas_call(
        known,
        name="known",
        in_specs=[smem] + vmem(5),
        out_specs=vmem(4),
        out_shape=(plane, plane, plane, array((8, CELLS), F32)),
        compiler_params=params(),
        cost_estimate=cost(5),
    )(freq_order, strip, before, after, state, forcing)

    first, last = pl.pallas_call(
        edge_flux,
        name="edge_flux",
        in_specs=vmem(4),
        out_specs=vmem(2),
        out_shape=(array((4, CELLS), F32),) * 2,
        compiler_params=params(),
        cost_estimate=cost(1),
    )(edge, extra, depth, wet_mask)
    after_flux = lax.ppermute(first, "tile", to_last)
    before_flux = lax.ppermute(last, "tile", to_next)

    return pl.pallas_call(
        finish,
        name="finish",
        in_specs=vmem(8 + 2 * RING),
        out_specs=vmem(1)[0],
        out_shape=array((1, 3, 4, CELLS, CELLS), F32),
        compiler_params=params(),
        cost_estimate=cost(5),
    )(extra, before_flux, after_flux, depth, wet_mask, east, north, eta, *upper_back, *lower_back)


def solution(mesh):
    in_specs = (
        P("sec", None, "harm", "tile", None),
        P("sec", None, "harm", "tile", None),
        P("sec", "tile", None),
        P("sec", "tile", None),
        P("tile"),
        P(),
    )
    out_specs = P("sec", None, "harm", "tile", None)
    return jax.shard_map(body, mesh=mesh, in_specs=in_specs, out_specs=out_specs, check_vma=False)
```

```python
import functools

import jax
import jax.numpy as jnp
from jax import lax
from jax.experimental import pallas as pl
from jax.experimental.pallas import tpu as pltpu
from jax.sharding import PartitionSpec as P

K = 8
NT = 64
CELLS = 256
RING = 4
LANES = 128
UPPER = 32
LOWER = 32
ROWS_UP = RING * UPPER
ROWS_LOW = RING * LOWER
REACH = 16
relax_step = 0.3
speed_floor = 0.01
omega_step = 0.1
TURN = 6.283185307179586 / NT
F32 = jnp.float32
BF16 = jnp.bfloat16
I32 = jnp.int32
MIB = 1 << 20


def params(mib=48):
    return pltpu.CompilerParams(vmem_limit_bytes=mib * MIB)


def cost(us):
    return pl.CostEstimate(flops=0, bytes_accessed=int(us * 3.0e6), transcendentals=0)


def vmem(count):
    return [pl.BlockSpec(memory_space=pltpu.VMEM)] * count


def dot(a, b):
    return jnp.dot(a, b, preferred_element_type=F32)


def pair(x):
    high = x.astype(BF16)
    return high, (x - high.astype(F32)).astype(BF16)


def iota(shape, dim):
    return lax.broadcasted_iota(I32, shape, dim)


def trig(freq_ref, me, time, slot, channel):
    owner = (me - slot + RING) & (RING - 1)
    constituent = owner * 2 + (channel >> 1)
    cycles = jnp.zeros(time.shape, I32)
    for k in range(K):
        cycles = jnp.where(constituent == k, freq_ref[k] + 1, cycles)
    angle = ((time * cycles) & (NT - 1)).astype(F32) * TURN
    return jnp.where((channel & 1) == 0, jnp.cos(angle), jnp.sin(angle))


def prepare(freq_ref, index_ref, fields_ref, strip_ref, forward_ref, backward_ref):
    me = lax.axis_index("harm")
    index = index_ref[...]
    row_of, col_of = index >> 8, index & (CELLS - 1)
    pick = jnp.where(iota((CELLS, CELLS), 0) == col_of, 1.0, 0.0).astype(BF16)
    picks = jnp.concatenate([pick, pick, pick], 0)
    at_row = iota((CELLS, CELLS), 0) == row_of
    for k in range(12):
        plane = fields_ref[k]
        high, rest = plane.astype(BF16), None
        rest = plane - high.astype(F32)
        mid, low = pair(rest)
        column = dot(jnp.concatenate([high, mid, low], 1), picks)
        strip_ref[k : k + 1, :] = jnp.sum(jnp.where(at_row, column, 0.0), axis=0, keepdims=True)
    shape = (128, 96)
    row, col = iota(shape, 0), iota(shape, 1)
    part, lane = col >> 5, col & 31
    value = trig(freq_ref, me, row & 63, lane >> 3, lane & 3)
    value = jnp.where((row >> 6) == ((lane >> 2) & 1), value, 0.0)
    high = value.astype(BF16).astype(F32)
    forward_ref[...] = jnp.where(part == 1, value - high, high).astype(BF16)
    shape = (64, 256)
    row, col = iota(shape, 0), iota(shape, 1)
    lane = row & 31
    value = trig(freq_ref, me, col & 63, lane >> 3, lane & 3) * (1.0 / NT)
    value = jnp.where(((col >> 6) & 1) == ((lane >> 2) & 1), value, 0.0)
    high = value.astype(BF16).astype(F32)
    low = jnp.where(col < 128, value - high, 0.0)
    backward_ref[...] = jnp.where(row < 32, high, low).astype(BF16)


def piece(state_ref, out_ref, sem, row, size, j):
    return pltpu.make_async_copy(
        state_ref.at[0, pl.ds(1, 2), :, pl.ds(row, size), pl.ds(j * LANES, LANES)],
        out_ref.reshape(2, 4, size, LANES),
        sem,
    )


def pack_upper(state_ref, *refs):
    outs, sems = refs[:RING], refs[RING]
    me = lax.axis_index("harm")
    copies = []
    for slot in (1, 3, 2, 0):
        row = pl.multiple_of(((me + slot) & (RING - 1)) * UPPER, UPPER)
        for j in range(2):
            out_ref = outs[slot].at[pl.ds(8 * UPPER * j, 8 * UPPER), :]
            copies.append(piece(state_ref, out_ref, sems.at[slot, j], row, UPPER, j))
    for copy in copies:
        copy.start()
    for copy in copies:
        copy.wait()


def pack_lower(strip_ref, state_ref, *refs):
    outs, (first_ref, last_ref, edges, sems, edge_sems) = refs[:RING], refs[RING:]
    me = lax.axis_index("harm")
    shelf = lax.axis_index("sec") == 1
    copies = []
    for e, row in enumerate((0, CELLS - 8)):
        copies.append(
            pltpu.make_async_copy(state_ref.at[0, :, :, pl.ds(row, 8), :], edges.at[e], edge_sems.at[e])
        )
    for slot in range(RING):
        row = pl.multiple_of(ROWS_UP + ((me + slot) & (RING - 1)) * LOWER, 8)
        for j in range(2):
            out_ref = outs[slot].at[pl.ds(8 * LOWER * j, 8 * LOWER), :]
            copies.append(piece(state_ref, out_ref, sems.at[slot, j], row, LOWER, j))
    for copy in copies:
        copy.start()
    for copy in copies[:2]:
        copy.wait()
    strip = strip_ref[...]
    take = jnp.logical_and(iota((12, CELLS), 1) == 0, shelf)
    first = edges[0].reshape(12, 8, CELLS)[:, 0, :]
    last = edges[1].reshape(12, 8, CELLS)[:, 7, :]
    first = jnp.where(take, strip[:, 0:1], first)
    last = jnp.where(take, strip[:, CELLS - 1 : CELLS], last)
    first_ref[...] = first[0:4]
    last_ref[...] = last[0:4]
    for e, values in enumerate((strip, first, last)):
        for j in range(2):
            row = 16 * LOWER + 24 * j + 8 * e
            for out_ref in outs:
                out_ref[row : row + 8, :] = values[4:12, j * LANES : (j + 1) * LANES]
    for copy in copies[2:]:
        copy.wait()


def terms(forward, backward, x):
    high, low = pair(x)
    samples = dot(forward, jnp.concatenate([high, high, low], 0))
    east, north = samples[:NT], samples[NT:]
    square = east * east + north * north + speed_floor
    speed = square * lax.rsqrt(square)
    high, low = pair(jnp.concatenate([speed * east, speed * north], 0))
    both = dot(backward, jnp.concatenate([high, low], 0))
    return both[:32] + both[32:]


def rows_terms(size, forward, backward, xs, outs):
    def step(r, carry):
        rows = [pl.ds(8 * size * j + r, 8, stride=size) for j in range(2)]
        halves = [jnp.concatenate([ref[rows[j], :] for ref in xs], 0) for j in range(2)]
        out = terms(forward, backward, jnp.concatenate(halves, 1))
        for slot in range(RING):
            for j in range(2):
                outs[slot][rows[j], :] = out[8 * slot : 8 * slot + 8, j * LANES : (j + 1) * LANES]
        return carry

    lax.fori_loop(0, size, step, 0, unroll=4)


def friction_upper(forward_ref, backward_ref, behind_ref, *refs):
    rows_terms(UPPER, forward_ref[...], backward_ref[...], refs[:RING], refs[RING:])


def friction_lower(forward_ref, backward_ref, behind_ref, *refs):
    xs, outs, extra_ref = refs[:RING], refs[RING : 2 * RING], refs[2 * RING]
    forward, backward = forward_ref[...], backward_ref[...]
    rows_terms(LOWER, forward, backward, xs, outs)
    for e in range(3):
        rows = [pl.ds(16 * LOWER + 24 * j + 8 * e, 8) for j in range(2)]
        halves = [jnp.concatenate([ref[rows[j], :] for ref in xs], 0) for j in range(2)]
        extra_ref[8 * e : 8 * e + 8, :] = terms(forward, backward, jnp.concatenate(halves, 1))[:8]


def left_right(x):
    lane = iota(x.shape, 1)
    right = jnp.where(lane == CELLS - 1, 0.0, pltpu.roll(x, CELLS - 1, 1))
    left = jnp.where(lane == 0, 0.0, pltpu.roll(x, 1, 1))
    return right - left


def up_down(x, before, after):
    count = x.shape[0]
    row = iota(x.shape, 0)
    down = jnp.where(row == count - 1, after, pltpu.roll(x, count - 1, 0))
    up = jnp.where(row == 0, before, pltpu.roll(x, 1, 0))
    return down - up


def known(freq_ref, strip_ref, before_ref, after_ref, state_ref, forcing_ref, east_ref, north_ref, eta_ref, edge_ref):
    me = lax.axis_index("harm")
    shelf = lax.axis_index("sec") == 1
    take = jnp.logical_and(iota((CELLS, CELLS), 1) == 0, shelf)
    columns = jnp.concatenate([strip_ref[...], jnp.zeros((4, CELLS), F32)], 0).T

    def field(f, ch):
        k = 4 * f + ch
        return jnp.where(take, columns[:, k : k + 1], state_ref[0, f, ch])

    for i in range(2):
        omega = omega_step * (freq_ref[2 * me + i] + 1).astype(F32)
        eta = [field(0, 2 * i + p) for p in range(2)]
        for p in range(2):
            ch = 2 * i + p
            turn = -omega if p else omega
            eta_ref[ch] = eta[p] - relax_step * (turn * eta[1 - p])
        east = [field(1, 2 * i + p) for p in range(2)]
        for p in range(2):
            ch = 2 * i + p
            turn = -omega if p else omega
            rest = turn * east[1 - p] + 0.5 * left_right(eta[p]) - forcing_ref[0, 0, ch]
            east_ref[ch] = east[p] - relax_step * rest
        north = [field(2, 2 * i + p) for p in range(2)]
        for p in range(2):
            ch = 2 * i + p
            turn = -omega if p else omega
            slope = up_down(eta[p], before_ref[ch : ch + 1, :], after_ref[ch : ch + 1, :])
            rest = turn * north[1 - p] + 0.5 * slope - forcing_ref[0, 1, ch]
            value = north[p] - relax_step * rest
            north_ref[ch] = value
            edge_ref[ch : ch + 1, :] = value[0:1, :]
            edge_ref[4 + ch : 5 + ch, :] = value[CELLS - 1 : CELLS, :]


def edge_flux(edge_ref, extra_ref, depth_ref, wet_ref, first_ref, last_ref):
    for out_ref, at, row in ((first_ref, 0, 0), (last_ref, 1, CELLS - 1)):
        height = depth_ref[0, row : row + 1, :]
        wet = wet_ref[0, row : row + 1, :].astype(F32)
        drag = extra_ref[8 + 8 * at + 4 : 8 + 8 * at + 8, :]
        north = wet * (edge_ref[4 * at : 4 * at + 4, :] - (relax_step / height) * drag)
        out_ref[...] = height * north


def transports(start, size, turned, extra_ref, depth_ref, wet_ref, sources, drags, store):
    me = lax.axis_index("harm")
    shelf = lax.axis_index("sec") == 1
    take = jnp.logical_and(iota((size, LANES), 1) == 0, shelf)
    turned[...] = extra_ref[0:8, :].T
    for slot in range(RING):
        at = pl.multiple_of(((me + slot) & (RING - 1)) * size, 8)
        rows = pl.ds(start + at, size)
        columns = turned[rows, :]
        wet = wet_ref[0, rows, :].astype(F32)
        factor = relax_step / depth_ref[0, rows, :]
        for k in range(8):
            left, right = (
                drags[slot][pl.ds((8 * j + k) * size, size), :] for j in range(2)
            )
            left = jnp.where(take, columns[:, k : k + 1], left)
            drag = jnp.concatenate([left, right], 1)
            store(1 + k // 4, k % 4, at, wet * (sources[k // 4][k % 4, rows, :] - factor * drag))


def new_eta(east, north, before, after, height, wet, eta):
    slope = left_right(height * east) + up_down(height * north, before, after)
    return wet * (eta - (0.5 * relax_step) * slope)


def finish_upper(extra_ref, depth_ref, wet_ref, east_ref, north_ref, eta_ref, *refs):
    slots, (out_ref, carry_ref, made, turned, sems) = refs[:RING], refs[RING:]

    def store(f, ch, row, value):
        made[f, ch, pl.ds(row, UPPER), :] = value

    transports(0, UPPER, turned, extra_ref, depth_ref, wet_ref, (east_ref, north_ref), slots, store)
    copies = []
    for f in (1, 2, 0):
        if f == 0:
            height = depth_ref[0, :ROWS_UP, :]
            wet = wet_ref[0, :ROWS_UP, :].astype(F32)
            for ch in range(4):
                made[0, ch] = new_eta(made[1, ch], made[2, ch], 0.0, 0.0, height, wet, eta_ref[ch, :ROWS_UP, :])
        copy = pltpu.make_async_copy(made.at[f], out_ref.at[0, f, :, pl.ds(0, ROWS_UP), :], sems.at[f])
        copy.start()
        copies.append(copy)
    for f in range(2):
        for ch in range(4):
            carry_ref[f, ch, :REACH, :] = made[1 + f, ch, :REACH, :]
            carry_ref[f, ch, REACH:, :] = made[1 + f, ch, ROWS_UP - REACH :, :]
    for copy in copies:
        copy.wait()


def finish_lower(
    extra_ref, before_ref, after_ref, depth_ref, wet_ref, east_ref, north_ref, eta_ref, carry_ref, begun_ref, *refs
):
    slots, (out_ref, made, level, top, turned, sems, level_sems) = refs[:RING], refs[RING:]
    top_row = ROWS_UP - REACH
    for f in range(2):
        for ch in range(4):
            made[f, ch, :REACH, :] = carry_ref[f, ch, REACH:, :]

    def store(f, ch, row, value):
        made[f - 1, ch, pl.ds(REACH + row, LOWER), :] = value

    transports(ROWS_UP, LOWER, turned, extra_ref, depth_ref, wet_ref, (east_ref, north_ref), slots, store)
    copies = []

    def send(source, target, sem):
        copy = pltpu.make_async_copy(source, target, sem)
        copy.start()
        copies.append(copy)

    for f in range(2):
        send(
            made.at[f, :, pl.ds(REACH, ROWS_LOW), :],
            out_ref.at[0, 1 + f, :, pl.ds(ROWS_UP, ROWS_LOW), :],
            sems.at[f],
        )
    height = depth_ref[0, :REACH, :]
    wet = wet_ref[0, :REACH, :].astype(F32)
    for ch in range(4):
        value = new_eta(
            carry_ref[0, ch, :REACH, :], carry_ref[1, ch, :REACH, :], before_ref[ch : ch + 1, :], 0.0,
            height, wet, eta_ref[ch, :REACH, :],
        )
        top[ch] = value[:8]
    send(top, out_ref.at[0, 0, :, pl.ds(0, 8), :], sems.at[2])
    height = depth_ref[0, top_row:, :]
    wet = wet_ref[0, top_row:, :].astype(F32)
    for ch in range(4):
        level[ch] = new_eta(
            made[0, ch], made[1, ch], 0.0, after_ref[ch : ch + 1, :], height, wet, eta_ref[ch, top_row:, :]
        )
        send(
            level.at[ch, pl.ds(8, ROWS_LOW + REACH - 8), :],
            out_ref.at[0, 0, ch, pl.ds(top_row + 8, ROWS_LOW + REACH - 8), :],
            level_sems.at[ch],
        )
    for copy in copies:
        copy.wait()


def around(value, steps):
    return lax.ppermute(value, "harm", [(i, (i + steps) % RING) for i in range(RING)])


def body(state, forcing, depth, wet_mask, nest_index, freq_order):
    me = lax.axis_index("harm")
    tiles = lax.axis_size("tile")
    smem = pl.BlockSpec(memory_space=pltpu.SMEM)
    hbm = pl.BlockSpec(memory_space=pl.ANY)
    main = pl.BlockSpec(memory_space=pltpu.HBM)
    array = jax.ShapeDtypeStruct

    upper = array((16 * UPPER, LANES), F32)
    parts = pl.pallas_call(
        pack_upper,
        name="pack_upper",
        in_specs=[hbm],
        out_specs=vmem(RING),
        out_shape=(upper,) * RING,
        scratch_shapes=[pltpu.SemaphoreType.DMA((RING, 2))],
        compiler_params=params(),
        cost_estimate=cost(2),
    )(state)
    raw = [parts[0]] + [around(parts[slot], slot) for slot in (1, 2, 3)]

    strip, forward, backward = pl.pallas_call(
        prepare,
        name="prepare",
        in_specs=[smem] + vmem(2),
        out_specs=vmem(3),
        out_shape=(array((12, CELLS), F32), array((128, 96), BF16), array((64, 256), BF16)),
        compiler_params=params(),
        cost_estimate=cost(4),
    )(freq_order, nest_index.reshape(1, CELLS), state.reshape(12, CELLS, CELLS))
    strip = lax.ppermute(strip, "sec", [(0, 1)])

    edge_eta = array((4, CELLS), F32)
    packed = pl.pallas_call(
        pack_lower,
        name="pack_lower",
        in_specs=vmem(1) + [hbm],
        out_specs=vmem(RING + 2),
        out_shape=(array((16 * LOWER + 48, LANES), F32),) * RING + (edge_eta, edge_eta),
        scratch_shapes=[
            pltpu.VMEM((2, 3, 4, 8, CELLS), F32),
            pltpu.SemaphoreType.DMA((RING, 2)),
            pltpu.SemaphoreType.DMA((2,)),
        ],
        compiler_params=params(),
        cost_estimate=cost(2),
    )(strip, state)
    first, last = packed[RING:]
    raw_lower = [packed[0]] + [around(packed[slot], slot) for slot in (1, 2, 3)]
    to_next = [(i, i + 1) for i in range(tiles - 1)]
    to_last = [(i + 1, i) for i in range(tiles - 1)]
    after = lax.ppermute(first, "tile", to_last)
    before = lax.ppermute(last, "tile", to_next)

    plane = array((4, CELLS, CELLS), F32)
    east, north, eta, edge = pl.pallas_call(
        known,
        name="known",
        in_specs=[smem] + vmem(5),
        out_specs=vmem(4),
        out_shape=(plane, plane, plane, array((8, CELLS), F32)),
        compiler_params=params(),
        cost_estimate=cost(5),
    )(freq_order, strip, before, after, state, forcing)

    made = pl.pallas_call(
        friction_upper,
        name="friction_upper",
        in_specs=vmem(2) + [hbm] + vmem(RING),
        out_specs=vmem(RING),
        out_shape=(upper,) * RING,
        compiler_params=params(),
        cost_estimate=cost(4),
    )(forward, backward, edge, *raw)
    drags = [made[0]] + [around(made[slot], -slot) for slot in (1, 2, 3)]
    made = pl.pallas_call(
        friction_lower,
        name="friction_lower",
        in_specs=vmem(2) + [hbm] + vmem(RING),
        out_specs=vmem(RING + 1),
        out_shape=(array((16 * LOWER, LANES), F32),) * RING + (array((24, CELLS), F32),),
        compiler_params=params(),
        cost_estimate=cost(4),
    )(forward, backward, made[0], *raw_lower)
    extra = made[RING]
    drags_lower = [made[0]] + [around(made[slot], -slot) for slot in (1, 2, 3)]

    first, last = pl.pallas_call(
        edge_flux,
        name="edge_flux",
        in_specs=vmem(4),
        out_specs=vmem(2),
        out_shape=(edge_eta, edge_eta),
        compiler_params=params(),
        cost_estimate=cost(1),
    )(edge, extra, depth, wet_mask)
    after_flux = lax.ppermute(first, "tile", to_last)
    before_flux = lax.ppermute(last, "tile", to_next)

    whole = array((1, 3, 4, CELLS, CELLS), F32)
    begun, carry = pl.pallas_call(
        finish_upper,
        name="finish_upper",
        in_specs=vmem(6 + RING),
        out_specs=[hbm, vmem(1)[0]],
        out_shape=(whole, array((2, 4, 2 * REACH, CELLS), F32)),
        scratch_shapes=[
            pltpu.VMEM((3, 4, ROWS_UP, CELLS), F32),
            pltpu.VMEM((CELLS, 8), F32),
            pltpu.SemaphoreType.DMA((3,)),
        ],
        compiler_params=params(),
        cost_estimate=cost(3),
    )(extra, depth, wet_mask, east, north, eta, *drags)
    return pl.pallas_call(
        finish_lower,
        name="finish_lower",
        in_specs=vmem(9) + [hbm] + vmem(RING),
        out_specs=hbm,
        out_shape=whole,
        input_output_aliases={9: 0},
        scratch_shapes=[
            pltpu.VMEM((2, 4, REACH + ROWS_LOW, CELLS), F32),
            pltpu.VMEM((4, REACH + ROWS_LOW, CELLS), F32),
            pltpu.VMEM((4, 8, CELLS), F32),
            pltpu.VMEM((CELLS, 8), F32),
            pltpu.SemaphoreType.DMA((3,)),
            pltpu.SemaphoreType.DMA((4,)),
        ],
        compiler_params=params(),
        cost_estimate=cost(3),
    )(extra, before_flux, after_flux, depth, wet_mask, east, north, eta, carry, begun, *drags_lower)


def solution(mesh):
    in_specs = (
        P("sec", None, "harm", "tile", None),
        P("sec", None, "harm", "tile", None),
        P("sec", "tile", None),
        P("sec", "tile", None),
        P("tile"),
        P(),
    )
    out_specs = P("sec", None, "harm", "tile", None)
    return jax.shard_map(body, mesh=mesh, in_specs=in_specs, out_specs=out_specs, check_vma=False)
```

```python
import functools

import jax
import jax.numpy as jnp
from jax import lax
from jax.experimental import pallas as pl
from jax.experimental.pallas import tpu as pltpu
from jax.sharding import PartitionSpec as P

K = 8
NT = 64
CELLS = 256
RING = 4
LANES = 128
UPPER = 32
LOWER = 32
ROWS_UP = RING * UPPER
ROWS_LOW = RING * LOWER
REACH = 16
relax_step = 0.3
speed_floor = 0.01
omega_step = 0.1
TURN = 6.283185307179586 / NT
F32 = jnp.float32
BF16 = jnp.bfloat16
I32 = jnp.int32
MIB = 1 << 20


def params(mib=48):
    return pltpu.CompilerParams(vmem_limit_bytes=mib * MIB)


def cost(us):
    return pl.CostEstimate(flops=0, bytes_accessed=int(us * 3.0e6), transcendentals=0)


def vmem(count):
    return [pl.BlockSpec(memory_space=pltpu.VMEM)] * count


def dot(a, b):
    return jnp.dot(a, b, preferred_element_type=F32)


def pair(x):
    high = x.astype(BF16)
    return high, (x - high.astype(F32)).astype(BF16)


def iota(shape, dim):
    return lax.broadcasted_iota(I32, shape, dim)


def trig(freq_ref, me, time, slot, channel):
    owner = (me - slot + RING) & (RING - 1)
    constituent = owner * 2 + (channel >> 1)
    cycles = jnp.zeros(time.shape, I32)
    for k in range(K):
        cycles = jnp.where(constituent == k, freq_ref[k] + 1, cycles)
    angle = ((time * cycles) & (NT - 1)).astype(F32) * TURN
    return jnp.where((channel & 1) == 0, jnp.cos(angle), jnp.sin(angle))


def prepare(freq_ref, index_ref, fields_ref, strip_ref, forward_ref, backward_ref):
    me = lax.axis_index("harm")
    index = index_ref[...]
    row_of, col_of = index >> 8, index & (CELLS - 1)
    pick = jnp.where(iota((CELLS, CELLS), 0) == col_of, 1.0, 0.0).astype(BF16)
    picks = jnp.concatenate([pick, pick, pick], 0)
    at_row = iota((CELLS, CELLS), 0) == row_of
    for k in range(12):
        plane = fields_ref[k]
        high, rest = plane.astype(BF16), None
        rest = plane - high.astype(F32)
        mid, low = pair(rest)
        column = dot(jnp.concatenate([high, mid, low], 1), picks)
        strip_ref[k : k + 1, :] = jnp.sum(jnp.where(at_row, column, 0.0), axis=0, keepdims=True)
    shape = (128, 96)
    row, col = iota(shape, 0), iota(shape, 1)
    part, lane = col >> 5, col & 31
    value = trig(freq_ref, me, row & 63, lane >> 3, lane & 3)
    value = jnp.where((row >> 6) == ((lane >> 2) & 1), value, 0.0)
    high = value.astype(BF16).astype(F32)
    forward_ref[...] = jnp.where(part == 1, value - high, high).astype(BF16)
    shape = (64, 256)
    row, col = iota(shape, 0), iota(shape, 1)
    lane = row & 31
    value = trig(freq_ref, me, col & 63, lane >> 3, lane & 3) * (1.0 / NT)
    value = jnp.where(((col >> 6) & 1) == ((lane >> 2) & 1), value, 0.0)
    high = value.astype(BF16).astype(F32)
    low = jnp.where(col < 128, value - high, 0.0)
    backward_ref[...] = jnp.where(row < 32, high, low).astype(BF16)


def piece(state_ref, field, out_ref, sem, row, size, j):
    return pltpu.make_async_copy(
        state_ref.at[0, pl.ds(field, 2), :, pl.ds(row, size), pl.ds(j * LANES, LANES)],
        out_ref.reshape(2, 4, size, LANES),
        sem,
    )


def pack_upper(state_ref, *refs):
    outs, sems = refs[:RING], refs[RING]
    me = lax.axis_index("harm")
    copies = []
    for slot in (1, 3, 2, 0):
        row = pl.multiple_of(((me + slot) & (RING - 1)) * UPPER, UPPER)
        for j in range(2):
            out_ref = outs[slot].at[pl.ds(8 * UPPER * j, 8 * UPPER), :]
            copies.append(piece(state_ref, 0, out_ref, sems.at[slot, j], row, UPPER, j))
    for copy in copies:
        copy.start()
    for copy in copies:
        copy.wait()


def pack_lower(strip_ref, state_ref, *refs):
    outs, (first_ref, last_ref, edges, sems, edge_sems) = refs[:RING], refs[RING:]
    me = lax.axis_index("harm")
    shelf = lax.axis_index("sec") == 1
    copies = []
    for e, row in enumerate((0, CELLS - 8)):
        copies.append(
            pltpu.make_async_copy(state_ref.at[0, :, :, pl.ds(row, 8), :], edges.at[e], edge_sems.at[e])
        )
    for slot in range(RING):
        row = pl.multiple_of(ROWS_UP + ((me + slot) & (RING - 1)) * LOWER, 8)
        for j in range(2):
            out_ref = outs[slot].at[pl.ds(8 * LOWER * j, 8 * LOWER), :]
            copies.append(piece(state_ref, 1, out_ref, sems.at[slot, j], row, LOWER, j))
    for copy in copies:
        copy.start()
    for copy in copies[:2]:
        copy.wait()
    strip = strip_ref[...]
    take = jnp.logical_and(iota((12, CELLS), 1) == 0, shelf)
    first = edges[0].reshape(12, 8, CELLS)[:, 0, :]
    last = edges[1].reshape(12, 8, CELLS)[:, 7, :]
    first = jnp.where(take, strip[:, 0:1], first)
    last = jnp.where(take, strip[:, CELLS - 1 : CELLS], last)
    first_ref[...] = first[0:4]
    last_ref[...] = last[0:4]
    for e, values in enumerate((strip, first, last)):
        for j in range(2):
            row = 16 * LOWER + 24 * j + 8 * e
            for out_ref in outs:
                out_ref[row : row + 8, :] = values[4:12, j * LANES : (j + 1) * LANES]
    for copy in copies[2:]:
        copy.wait()


def terms(forward, backward, x):
    high, low = pair(x)
    samples = dot(forward, jnp.concatenate([high, high, low], 0))
    east, north = samples[:NT], samples[NT:]
    square = east * east + north * north + speed_floor
    speed = square * lax.rsqrt(square)
    high, low = pair(jnp.concatenate([speed * east, speed * north], 0))
    both = dot(backward, jnp.concatenate([high, low], 0))
    return both[:32] + both[32:]


def rows_terms(size, forward, backward, xs, outs):
    def step(r, carry):
        rows = [pl.ds(8 * size * j + r, 8, stride=size) for j in range(2)]
        halves = [jnp.concatenate([ref[rows[j], :] for ref in xs], 0) for j in range(2)]
        out = terms(forward, backward, jnp.concatenate(halves, 1))
        for slot in range(RING):
            for j in range(2):
                outs[slot][rows[j], :] = out[8 * slot : 8 * slot + 8, j * LANES : (j + 1) * LANES]
        return carry

    lax.fori_loop(0, size, step, 0, unroll=4)


def friction_upper(forward_ref, backward_ref, first_ref, last_ref, *refs):
    rows_terms(UPPER, forward_ref[...], backward_ref[...], refs[:RING], refs[RING : 2 * RING])
    refs[2 * RING][...] = first_ref[...]
    refs[2 * RING + 1][...] = last_ref[...]


def friction_lower(forward_ref, backward_ref, behind_ref, *refs):
    xs, outs, extra_ref = refs[:RING], refs[RING : 2 * RING], refs[2 * RING]
    forward, backward = forward_ref[...], backward_ref[...]
    rows_terms(LOWER, forward, backward, xs, outs)
    for e in range(3):
        rows = [pl.ds(16 * LOWER + 24 * j + 8 * e, 8) for j in range(2)]
        halves = [jnp.concatenate([ref[rows[j], :] for ref in xs], 0) for j in range(2)]
        extra_ref[8 * e : 8 * e + 8, :] = terms(forward, backward, jnp.concatenate(halves, 1))[:8]


def left_right(x):
    lane = iota(x.shape, 1)
    right = jnp.where(lane == CELLS - 1, 0.0, pltpu.roll(x, CELLS - 1, 1))
    left = jnp.where(lane == 0, 0.0, pltpu.roll(x, 1, 1))
    return right - left


def up_down(x, before, after):
    count = x.shape[0]
    row = iota(x.shape, 0)
    down = jnp.where(row == count - 1, after, pltpu.roll(x, count - 1, 0))
    up = jnp.where(row == 0, before, pltpu.roll(x, 1, 0))
    return down - up


def known(freq_ref, behind_ref, strip_ref, state_ref, forcing_ref, east_ref, north_ref, eta_ref, edge_ref):
    me = lax.axis_index("harm")
    shelf = lax.axis_index("sec") == 1
    take = jnp.logical_and(iota((CELLS, CELLS), 1) == 0, shelf)
    columns = jnp.concatenate([strip_ref[...], jnp.zeros((4, CELLS), F32)], 0).T

    def field(f, ch):
        k = 4 * f + ch
        return jnp.where(take, columns[:, k : k + 1], state_ref[0, f, ch])

    for i in range(2):
        omega = omega_step * (freq_ref[2 * me + i] + 1).astype(F32)
        eta = [field(0, 2 * i + p) for p in range(2)]
        for p in range(2):
            ch = 2 * i + p
            turn = -omega if p else omega
            eta_ref[ch] = eta[p] - relax_step * (turn * eta[1 - p])
        east = [field(1, 2 * i + p) for p in range(2)]
        for p in range(2):
            ch = 2 * i + p
            turn = -omega if p else omega
            rest = turn * east[1 - p] + 0.5 * left_right(eta[p]) - forcing_ref[0, 0, ch]
            east_ref[ch] = east[p] - relax_step * rest
        north = [field(2, 2 * i + p) for p in range(2)]
        for p in range(2):
            ch = 2 * i + p
            turn = -omega if p else omega
            slope = up_down(eta[p], 0.0, 0.0)
            rest = turn * north[1 - p] + 0.5 * slope - forcing_ref[0, 1, ch]
            value = north[p] - relax_step * rest
            north_ref[ch] = value
            edge_ref[ch : ch + 1, :] = value[0:1, :]
            edge_ref[4 + ch : 5 + ch, :] = value[CELLS - 1 : CELLS, :]


def edge_flux(edge_ref, before_ref, after_ref, extra_ref, depth_ref, wet_ref, first_ref, last_ref, north_ref):
    half = 0.5 * relax_step
    for out_ref, at, row, beside in (
        (first_ref, 0, 0, half * before_ref[...]),
        (last_ref, 1, CELLS - 1, -half * after_ref[...]),
    ):
        height = depth_ref[0, row : row + 1, :]
        wet = wet_ref[0, row : row + 1, :].astype(F32)
        drag = extra_ref[8 + 8 * at + 4 : 8 + 8 * at + 8, :]
        north = wet * (edge_ref[4 * at : 4 * at + 4, :] + beside - (relax_step / height) * drag)
        out_ref[...] = height * north
        north_ref[4 * at : 4 * at + 4, :] = north


def transports(start, size, turned, extra_ref, depth_ref, wet_ref, sources, drags, store):
    me = lax.axis_index("harm")
    shelf = lax.axis_index("sec") == 1
    take = jnp.logical_and(iota((size, LANES), 1) == 0, shelf)
    turned[...] = extra_ref[0:8, :].T
    for slot in range(RING):
        at = pl.multiple_of(((me + slot) & (RING - 1)) * size, 8)
        rows = pl.ds(start + at, size)
        columns = turned[rows, :]
        wet = wet_ref[0, rows, :].astype(F32)
        factor = relax_step / depth_ref[0, rows, :]
        for k in range(8):
            left, right = (
                drags[slot][pl.ds((8 * j + k) * size, size), :] for j in range(2)
            )
            left = jnp.where(take, columns[:, k : k + 1], left)
            drag = jnp.concatenate([left, right], 1)
            store(1 + k // 4, k % 4, at, wet * (sources[k // 4][k % 4, rows, :] - factor * drag))


def new_eta(east, north, before, after, height, wet, eta):
    slope = left_right(height * east) + up_down(height * north, before, after)
    return wet * (eta - (0.5 * relax_step) * slope)


def finish_upper(extra_ref, depth_ref, wet_ref, east_ref, north_ref, eta_ref, *refs):
    slots, (out_ref, carry_ref, made, turned, sems) = refs[:RING], refs[RING:]

    def store(f, ch, row, value):
        made[f, ch, pl.ds(row, UPPER), :] = value

    transports(0, UPPER, turned, extra_ref, depth_ref, wet_ref, (east_ref, north_ref), slots, store)
    copies = []
    for f in (1, 2, 0):
        if f == 0:
            height = depth_ref[0, :ROWS_UP, :]
            wet = wet_ref[0, :ROWS_UP, :].astype(F32)
            for ch in range(4):
                made[0, ch] = new_eta(made[1, ch], made[2, ch], 0.0, 0.0, height, wet, eta_ref[ch, :ROWS_UP, :])
        copy = pltpu.make_async_copy(made.at[f], out_ref.at[0, f, :, pl.ds(0, ROWS_UP), :], sems.at[f])
        copy.start()
        copies.append(copy)
    for f in range(2):
        for ch in range(4):
            carry_ref[f, ch, :REACH, :] = made[1 + f, ch, :REACH, :]
            carry_ref[f, ch, REACH:, :] = made[1 + f, ch, ROWS_UP - REACH :, :]
    for copy in copies:
        copy.wait()


def finish_lower(
    extra_ref, edge_ref, before_ref, after_ref, depth_ref, wet_ref, east_ref, north_ref, eta_ref, carry_ref, begun_ref, *refs
):
    slots, (out_ref, made, level, top, turned, sems, level_sems) = refs[:RING], refs[RING:]
    top_row = ROWS_UP - REACH
    for f in range(2):
        for ch in range(4):
            made[f, ch, :REACH, :] = carry_ref[f, ch, REACH:, :]

    def store(f, ch, row, value):
        made[f - 1, ch, pl.ds(REACH + row, LOWER), :] = value

    transports(ROWS_UP, LOWER, turned, extra_ref, depth_ref, wet_ref, (east_ref, north_ref), slots, store)
    for ch in range(4):
        made[1, ch, REACH + ROWS_LOW - 1 : REACH + ROWS_LOW, :] = edge_ref[4 + ch : 5 + ch, :]
    copies = []

    def send(source, target, sem):
        copy = pltpu.make_async_copy(source, target, sem)
        copy.start()
        copies.append(copy)

    for f in range(2):
        send(
            made.at[f, :, pl.ds(REACH, ROWS_LOW), :],
            out_ref.at[0, 1 + f, :, pl.ds(ROWS_UP, ROWS_LOW), :],
            sems.at[f],
        )
    height = depth_ref[0, :REACH, :]
    wet = wet_ref[0, :REACH, :].astype(F32)
    for ch in range(4):
        north = carry_ref[1, ch, :REACH, :]
        north = jnp.where(iota((REACH, CELLS), 0) == 0, edge_ref[ch : ch + 1, :], north)
        value = new_eta(
            carry_ref[0, ch, :REACH, :], north, before_ref[ch : ch + 1, :], 0.0, height, wet, eta_ref[ch, :REACH, :]
        )
        top[0, ch] = value[:8]
        top[1, ch] = north[:8]
    for i in range(2):
        send(top.at[i], out_ref.at[0, 2 * i, :, pl.ds(0, 8), :], sems.at[2 + i])
    height = depth_ref[0, top_row:, :]
    wet = wet_ref[0, top_row:, :].astype(F32)
    for ch in range(4):
        level[ch] = new_eta(
            made[0, ch], made[1, ch], 0.0, after_ref[ch : ch + 1, :], height, wet, eta_ref[ch, top_row:, :]
        )
        send(
            level.at[ch, pl.ds(8, ROWS_LOW + REACH - 8), :],
            out_ref.at[0, 0, ch, pl.ds(top_row + 8, ROWS_LOW + REACH - 8), :],
            level_sems.at[ch],
        )
    for copy in copies:
        copy.wait()


def around(value, steps):
    return lax.ppermute(value, "harm", [(i, (i + steps) % RING) for i in range(RING)])


def body(state, forcing, depth, wet_mask, nest_index, freq_order):
    me = lax.axis_index("harm")
    tiles = lax.axis_size("tile")
    smem = pl.BlockSpec(memory_space=pltpu.SMEM)
    hbm = pl.BlockSpec(memory_space=pl.ANY)
    main = pl.BlockSpec(memory_space=pltpu.HBM)
    array = jax.ShapeDtypeStruct

    upper = array((16 * UPPER, LANES), F32)
    parts = pl.pallas_call(
        pack_upper,
        name="pack_upper",
        in_specs=[hbm],
        out_specs=vmem(RING),
        out_shape=(upper,) * RING,
        scratch_shapes=[pltpu.SemaphoreType.DMA((RING, 2))],
        compiler_params=params(),
        cost_estimate=cost(2),
    )(lax.slice(state, (0, 1, 0, 0, 0), (1, 3, 4, ROWS_UP, CELLS)))
    raw = [parts[0]] + [around(parts[slot], slot) for slot in (1, 2, 3)]

    strip, forward, backward = pl.pallas_call(
        prepare,
        name="prepare",
        in_specs=[smem] + vmem(2),
        out_specs=vmem(3),
        out_shape=(array((12, CELLS), F32), array((128, 96), BF16), array((64, 256), BF16)),
        compiler_params=params(),
        cost_estimate=cost(4),
    )(freq_order, nest_index.reshape(1, CELLS), state.reshape(12, CELLS, CELLS))
    strip = lax.ppermute(strip, "sec", [(0, 1)])

    edge_eta = array((4, CELLS), F32)
    packed = pl.pallas_call(
        pack_lower,
        name="pack_lower",
        in_specs=vmem(1) + [hbm],
        out_specs=vmem(RING + 2),
        out_shape=(array((16 * LOWER + 48, LANES), F32),) * RING + (edge_eta, edge_eta),
        scratch_shapes=[
            pltpu.VMEM((2, 3, 4, 8, CELLS), F32),
            pltpu.SemaphoreType.DMA((RING, 2)),
            pltpu.SemaphoreType.DMA((2,)),
        ],
        compiler_params=params(),
        cost_estimate=cost(2),
    )(strip, state)
    first, last = packed[RING:]
    raw_lower = [packed[0]] + [around(packed[slot], slot) for slot in (1, 2, 3)]
    to_next = [(i, i + 1) for i in range(tiles - 1)]
    to_last = [(i + 1, i) for i in range(tiles - 1)]
    made = pl.pallas_call(
        friction_upper,
        name="friction_upper",
        in_specs=vmem(4 + RING),
        out_specs=vmem(RING + 2),
        out_shape=(upper,) * RING + (edge_eta, edge_eta),
        compiler_params=params(),
        cost_estimate=cost(4),
    )(forward, backward, first, last, *raw)
    after = lax.ppermute(made[RING], "tile", to_last)
    before = lax.ppermute(made[RING + 1], "tile", to_next)
    drags = [made[0]] + [around(made[slot], -slot) for slot in (1, 2, 3)]
    plane = array((4, CELLS, CELLS), F32)
    east, north, eta, edge = pl.pallas_call(
        known,
        name="known",
        in_specs=[smem, hbm] + vmem(3),
        out_specs=vmem(4),
        out_shape=(plane, plane, plane, array((8, CELLS), F32)),
        compiler_params=params(),
        cost_estimate=cost(5),
    )(freq_order, made[0], strip, state, forcing)

    made = pl.pallas_call(
        friction_lower,
        name="friction_lower",
        in_specs=vmem(2) + [hbm] + vmem(RING),
        out_specs=vmem(RING + 1),
        out_shape=(array((16 * LOWER, LANES), F32),) * RING + (array((24, CELLS), F32),),
        compiler_params=params(),
        cost_estimate=cost(4),
    )(forward, backward, edge, *raw_lower)
    extra = made[RING]
    drags_lower = [made[0]] + [around(made[slot], -slot) for slot in (1, 2, 3)]

    first, last, edge = pl.pallas_call(
        edge_flux,
        name="edge_flux",
        in_specs=vmem(6),
        out_specs=vmem(3),
        out_shape=(edge_eta, edge_eta, array((8, CELLS), F32)),
        compiler_params=params(),
        cost_estimate=cost(1),
    )(edge, before, after, extra, depth, wet_mask)
    after_flux = lax.ppermute(first, "tile", to_last)
    before_flux = lax.ppermute(last, "tile", to_next)

    whole = array((1, 3, 4, CELLS, CELLS), F32)
    begun, carry = pl.pallas_call(
        finish_upper,
        name="finish_upper",
        in_specs=vmem(6 + RING),
        out_specs=[hbm, vmem(1)[0]],
        out_shape=(whole, array((2, 4, 2 * REACH, CELLS), F32)),
        scratch_shapes=[
            pltpu.VMEM((3, 4, ROWS_UP, CELLS), F32),
            pltpu.VMEM((CELLS, 8), F32),
            pltpu.SemaphoreType.DMA((3,)),
        ],
        compiler_params=params(),
        cost_estimate=cost(3),
    )(extra, depth, wet_mask, east, north, eta, *drags)
    return pl.pallas_call(
        finish_lower,
        name="finish_lower",
        in_specs=vmem(10) + [hbm] + vmem(RING),
        out_specs=hbm,
        out_shape=whole,
        input_output_aliases={10: 0},
        scratch_shapes=[
            pltpu.VMEM((2, 4, REACH + ROWS_LOW, CELLS), F32),
            pltpu.VMEM((4, REACH + ROWS_LOW, CELLS), F32),
            pltpu.VMEM((2, 4, 8, CELLS), F32),
            pltpu.VMEM((CELLS, 8), F32),
            pltpu.SemaphoreType.DMA((4,)),
            pltpu.SemaphoreType.DMA((4,)),
        ],
        compiler_params=params(),
        cost_estimate=cost(3),
    )(extra, edge, before_flux, after_flux, depth, wet_mask, east, north, eta, carry, begun, *drags_lower)


def solution(mesh):
    in_specs = (
        P("sec", None, "harm", "tile", None),
        P("sec", None, "harm", "tile", None),
        P("sec", "tile", None),
        P("sec", "tile", None),
        P("tile"),
        P(),
    )
    out_specs = P("sec", None, "harm", "tile", None)
    return jax.shard_map(body, mesh=mesh, in_specs=in_specs, out_specs=out_specs, check_vma=False)
```

```python
import functools

import jax
import jax.numpy as jnp
from jax import lax
from jax.experimental import pallas as pl
from jax.experimental.pallas import tpu as pltpu
from jax.sharding import PartitionSpec as P

K = 8
NT = 64
CELLS = 256
RING = 4
LANES = 128
UPPER = 32
LOWER = 32
ROWS_UP = RING * UPPER
ROWS_LOW = RING * LOWER
REACH = 16
relax_step = 0.3
speed_floor = 0.01
omega_step = 0.1
TURN = 6.283185307179586 / NT
F32 = jnp.float32
BF16 = jnp.bfloat16
I32 = jnp.int32
MIB = 1 << 20


def params(mib=48):
    return pltpu.CompilerParams(vmem_limit_bytes=mib * MIB)


def cost(us):
    return pl.CostEstimate(flops=0, bytes_accessed=int(us * 3.0e6), transcendentals=0)


def vmem(count):
    return [pl.BlockSpec(memory_space=pltpu.VMEM)] * count


def dot(a, b):
    return jnp.dot(a, b, preferred_element_type=F32)


def pair(x):
    high = x.astype(BF16)
    return high, (x - high.astype(F32)).astype(BF16)


def iota(shape, dim):
    return lax.broadcasted_iota(I32, shape, dim)


def trig(freq_ref, me, time, slot, channel):
    owner = (me - slot + RING) & (RING - 1)
    constituent = owner * 2 + (channel >> 1)
    cycles = jnp.zeros(time.shape, I32)
    for k in range(K):
        cycles = jnp.where(constituent == k, freq_ref[k] + 1, cycles)
    angle = ((time * cycles) & (NT - 1)).astype(F32) * TURN
    return jnp.where((channel & 1) == 0, jnp.cos(angle), jnp.sin(angle))


def prepare(freq_ref, index_ref, fields_ref, strip_ref, forward_ref, backward_ref):
    me = lax.axis_index("harm")
    index = index_ref[...]
    row_of, col_of = index >> 8, index & (CELLS - 1)
    pick = jnp.where(iota((CELLS, CELLS), 0) == col_of, 1.0, 0.0).astype(BF16)
    picks = jnp.concatenate([pick, pick, pick], 0)
    at_row = iota((CELLS, CELLS), 0) == row_of
    for k in range(12):
        plane = fields_ref[k]
        high, rest = plane.astype(BF16), None
        rest = plane - high.astype(F32)
        mid, low = pair(rest)
        column = dot(jnp.concatenate([high, mid, low], 1), picks)
        strip_ref[k : k + 1, :] = jnp.sum(jnp.where(at_row, column, 0.0), axis=0, keepdims=True)
    shape = (128, 96)
    row, col = iota(shape, 0), iota(shape, 1)
    part, lane = col >> 5, col & 31
    value = trig(freq_ref, me, row & 63, lane >> 3, lane & 3)
    value = jnp.where((row >> 6) == ((lane >> 2) & 1), value, 0.0)
    high = value.astype(BF16).astype(F32)
    forward_ref[...] = jnp.where(part == 1, value - high, high).astype(BF16)
    shape = (64, 256)
    row, col = iota(shape, 0), iota(shape, 1)
    lane = row & 31
    value = trig(freq_ref, me, col & 63, lane >> 3, lane & 3) * (1.0 / NT)
    value = jnp.where(((col >> 6) & 1) == ((lane >> 2) & 1), value, 0.0)
    high = value.astype(BF16).astype(F32)
    low = jnp.where(col < 128, value - high, 0.0)
    backward_ref[...] = jnp.where(row < 32, high, low).astype(BF16)


def piece(state_ref, field, out_ref, sem, row, size, j):
    return pltpu.make_async_copy(
        state_ref.at[0, pl.ds(field, 2), :, pl.ds(row, size), pl.ds(j * LANES, LANES)],
        out_ref.reshape(2, 4, size, LANES),
        sem,
    )


def pack_upper(state_ref, *refs):
    outs, sems = refs[:RING], refs[RING]
    me = lax.axis_index("harm")
    copies = []
    for slot in (1, 3, 2, 0):
        row = pl.multiple_of(((me + slot) & (RING - 1)) * UPPER, UPPER)
        for j in range(2):
            out_ref = outs[slot].at[pl.ds(8 * UPPER * j, 8 * UPPER), :]
            copies.append(piece(state_ref, 0, out_ref, sems.at[slot, j], row, UPPER, j))
    for copy in copies:
        copy.start()
    for copy in copies:
        copy.wait()


def pack_lower(strip_ref, state_ref, *refs):
    outs, (first_ref, last_ref, edges, sems, edge_sems) = refs[:RING], refs[RING:]
    me = lax.axis_index("harm")
    shelf = lax.axis_index("sec") == 1
    copies = []
    for e, row in enumerate((0, CELLS - 8)):
        copies.append(
            pltpu.make_async_copy(state_ref.at[0, :, :, pl.ds(row, 8), :], edges.at[e], edge_sems.at[e])
        )
    for slot in range(RING):
        row = pl.multiple_of(ROWS_UP + ((me + slot) & (RING - 1)) * LOWER, 8)
        for j in range(2):
            out_ref = outs[slot].at[pl.ds(8 * LOWER * j, 8 * LOWER), :]
            copies.append(piece(state_ref, 1, out_ref, sems.at[slot, j], row, LOWER, j))
    for copy in copies:
        copy.start()
    for copy in copies[:2]:
        copy.wait()
    strip = strip_ref[...]
    take = jnp.logical_and(iota((12, CELLS), 1) == 0, shelf)
    first = edges[0].reshape(12, 8, CELLS)[:, 0, :]
    last = edges[1].reshape(12, 8, CELLS)[:, 7, :]
    first = jnp.where(take, strip[:, 0:1], first)
    last = jnp.where(take, strip[:, CELLS - 1 : CELLS], last)
    first_ref[...] = first[0:4]
    last_ref[...] = last[0:4]
    for e, values in enumerate((strip, first, last)):
        for j in range(2):
            row = 16 * LOWER + 24 * j + 8 * e
            for out_ref in outs:
                out_ref[row : row + 8, :] = values[4:12, j * LANES : (j + 1) * LANES]
    for copy in copies[2:]:
        copy.wait()


def terms(forward, backward, x):
    high, low = pair(x)
    samples = dot(forward, jnp.concatenate([high, high, low], 0))
    east, north = samples[:NT], samples[NT:]
    square = east * east + north * north + speed_floor
    speed = square * lax.rsqrt(square)
    high, low = pair(jnp.concatenate([speed * east, speed * north], 0))
    both = dot(backward, jnp.concatenate([high, low], 0))
    return both[:32] + both[32:]


def rows_terms(size, forward, backward, xs, outs):
    def step(r, carry):
        rows = [pl.ds(8 * size * j + r, 8, stride=size) for j in range(2)]
        halves = [jnp.concatenate([ref[rows[j], :] for ref in xs], 0) for j in range(2)]
        out = terms(forward, backward, jnp.concatenate(halves, 1))
        for slot in range(RING):
            for j in range(2):
                outs[slot][rows[j], :] = out[8 * slot : 8 * slot + 8, j * LANES : (j + 1) * LANES]
        return carry

    lax.fori_loop(0, size, step, 0, unroll=8)


def friction_upper(forward_ref, backward_ref, first_ref, last_ref, *refs):
    rows_terms(UPPER, forward_ref[...], backward_ref[...], refs[:RING], refs[RING : 2 * RING])
    refs[2 * RING][...] = first_ref[...]
    refs[2 * RING + 1][...] = last_ref[...]


def friction_lower(forward_ref, backward_ref, behind_ref, *refs):
    xs, outs, extra_ref = refs[:RING], refs[RING : 2 * RING], refs[2 * RING]
    forward, backward = forward_ref[...], backward_ref[...]
    rows_terms(LOWER, forward, backward, xs, outs)
    for e in range(3):
        rows = [pl.ds(16 * LOWER + 24 * j + 8 * e, 8) for j in range(2)]
        halves = [jnp.concatenate([ref[rows[j], :] for ref in xs], 0) for j in range(2)]
        extra_ref[8 * e : 8 * e + 8, :] = terms(forward, backward, jnp.concatenate(halves, 1))[:8]


def left_right(x):
    lane = iota(x.shape, 1)
    right = jnp.where(lane == CELLS - 1, 0.0, pltpu.roll(x, CELLS - 1, 1))
    left = jnp.where(lane == 0, 0.0, pltpu.roll(x, 1, 1))
    return right - left


def up_down(x, before, after):
    count = x.shape[0]
    row = iota(x.shape, 0)
    down = jnp.where(row == count - 1, after, pltpu.roll(x, count - 1, 0))
    up = jnp.where(row == 0, before, pltpu.roll(x, 1, 0))
    return down - up


def known(freq_ref, behind_ref, strip_ref, state_ref, forcing_ref, east_ref, north_ref, eta_ref, edge_ref):
    me = lax.axis_index("harm")
    shelf = lax.axis_index("sec") == 1
    take = jnp.logical_and(iota((CELLS, LANES), 1) == 0, shelf)
    columns = jnp.concatenate([strip_ref[...], jnp.zeros((4, CELLS), F32)], 0).T

    def field(f, ch):
        k = 4 * f + ch
        left = jnp.where(take, columns[:, k : k + 1], state_ref[0, f, ch, :, :LANES])
        return jnp.concatenate([left, state_ref[0, f, ch, :, LANES:]], 1)

    for i in range(2):
        omega = omega_step * (freq_ref[2 * me + i] + 1).astype(F32)
        eta = [field(0, 2 * i + p) for p in range(2)]
        for p in range(2):
            ch = 2 * i + p
            turn = -omega if p else omega
            eta_ref[ch] = eta[p] - relax_step * (turn * eta[1 - p])
        east = [field(1, 2 * i + p) for p in range(2)]
        for p in range(2):
            ch = 2 * i + p
            turn = -omega if p else omega
            rest = turn * east[1 - p] + 0.5 * left_right(eta[p]) - forcing_ref[0, 0, ch]
            east_ref[ch] = east[p] - relax_step * rest
        north = [field(2, 2 * i + p) for p in range(2)]
        for p in range(2):
            ch = 2 * i + p
            turn = -omega if p else omega
            slope = up_down(eta[p], 0.0, 0.0)
            rest = turn * north[1 - p] + 0.5 * slope - forcing_ref[0, 1, ch]
            value = north[p] - relax_step * rest
            north_ref[ch] = value
            edge_ref[ch : ch + 1, :] = value[0:1, :]
            edge_ref[4 + ch : 5 + ch, :] = value[CELLS - 1 : CELLS, :]


def edge_flux(edge_ref, before_ref, after_ref, extra_ref, depth_ref, wet_ref, first_ref, last_ref, north_ref):
    half = 0.5 * relax_step
    for out_ref, at, row, beside in (
        (first_ref, 0, 0, half * before_ref[...]),
        (last_ref, 1, CELLS - 1, -half * after_ref[...]),
    ):
        height = depth_ref[0, row : row + 1, :]
        wet = wet_ref[0, row : row + 1, :].astype(F32)
        drag = extra_ref[8 + 8 * at + 4 : 8 + 8 * at + 8, :]
        north = wet * (edge_ref[4 * at : 4 * at + 4, :] + beside - (relax_step / height) * drag)
        out_ref[...] = height * north
        north_ref[4 * at : 4 * at + 4, :] = north


def transports(start, size, turned, extra_ref, depth_ref, wet_ref, sources, drags, store):
    me = lax.axis_index("harm")
    shelf = lax.axis_index("sec") == 1
    take = jnp.logical_and(iota((size, LANES), 1) == 0, shelf)
    turned[...] = extra_ref[0:8, :].T
    for slot in range(RING):
        at = pl.multiple_of(((me + slot) & (RING - 1)) * size, 8)
        rows = pl.ds(start + at, size)
        columns = turned[rows, :]
        wet = wet_ref[0, rows, :].astype(F32)
        factor = relax_step / depth_ref[0, rows, :]
        for k in range(8):
            left, right = (
                drags[slot][pl.ds((8 * j + k) * size, size), :] for j in range(2)
            )
            left = jnp.where(take, columns[:, k : k + 1], left)
            drag = jnp.concatenate([left, right], 1)
            store(1 + k // 4, k % 4, at, wet * (sources[k // 4][k % 4, rows, :] - factor * drag))


def new_eta(east, north, before, after, height, wet, eta):
    slope = left_right(height * east) + up_down(height * north, before, after)
    return wet * (eta - (0.5 * relax_step) * slope)


def finish_upper(extra_ref, depth_ref, wet_ref, east_ref, north_ref, eta_ref, *refs):
    slots, (out_ref, carry_ref, made, turned, sems) = refs[:RING], refs[RING:]

    def store(f, ch, row, value):
        made[f, ch, pl.ds(row, UPPER), :] = value

    transports(0, UPPER, turned, extra_ref, depth_ref, wet_ref, (east_ref, north_ref), slots, store)
    copies = []
    for f in (1, 2, 0):
        if f == 0:
            height = depth_ref[0, :ROWS_UP, :]
            wet = wet_ref[0, :ROWS_UP, :].astype(F32)
            for ch in range(4):
                made[0, ch] = new_eta(made[1, ch], made[2, ch], 0.0, 0.0, height, wet, eta_ref[ch, :ROWS_UP, :])
        copy = pltpu.make_async_copy(made.at[f], out_ref.at[0, f, :, pl.ds(0, ROWS_UP), :], sems.at[f])
        copy.start()
        copies.append(copy)
    for f in range(2):
        for ch in range(4):
            carry_ref[f, ch, :REACH, :] = made[1 + f, ch, :REACH, :]
            carry_ref[f, ch, REACH:, :] = made[1 + f, ch, ROWS_UP - REACH :, :]
    for copy in copies:
        copy.wait()


def finish_lower(
    extra_ref, edge_ref, before_ref, after_ref, depth_ref, wet_ref, east_ref, north_ref, eta_ref, carry_ref, begun_ref, *refs
):
    slots, (out_ref, made, level, top, turned, sems, level_sems) = refs[:RING], refs[RING:]
    top_row = ROWS_UP - REACH
    for f in range(2):
        for ch in range(4):
            made[f, ch, :REACH, :] = carry_ref[f, ch, REACH:, :]

    def store(f, ch, row, value):
        made[f - 1, ch, pl.ds(REACH + row, LOWER), :] = value

    transports(ROWS_UP, LOWER, turned, extra_ref, depth_ref, wet_ref, (east_ref, north_ref), slots, store)
    for ch in range(4):
        made[1, ch, REACH + ROWS_LOW - 1 : REACH + ROWS_LOW, :] = edge_ref[4 + ch : 5 + ch, :]
    copies = []

    def send(source, target, sem):
        copy = pltpu.make_async_copy(source, target, sem)
        copy.start()
        copies.append(copy)

    for f in range(2):
        send(
            made.at[f, :, pl.ds(REACH, ROWS_LOW), :],
            out_ref.at[0, 1 + f, :, pl.ds(ROWS_UP, ROWS_LOW), :],
            sems.at[f],
        )
    height = depth_ref[0, :REACH, :]
    wet = wet_ref[0, :REACH, :].astype(F32)
    for ch in range(4):
        north = carry_ref[1, ch, :REACH, :]
        north = jnp.where(iota((REACH, CELLS), 0) == 0, edge_ref[ch : ch + 1, :], north)
        value = new_eta(
            carry_ref[0, ch, :REACH, :], north, before_ref[ch : ch + 1, :], 0.0, height, wet, eta_ref[ch, :REACH, :]
        )
        top[0, ch] = value[:8]
        top[1, ch] = north[:8]
    for i in range(2):
        send(top.at[i], out_ref.at[0, 2 * i, :, pl.ds(0, 8), :], sems.at[2 + i])
    height = depth_ref[0, top_row:, :]
    wet = wet_ref[0, top_row:, :].astype(F32)
    for ch in range(4):
        level[ch] = new_eta(
            made[0, ch], made[1, ch], 0.0, after_ref[ch : ch + 1, :], height, wet, eta_ref[ch, top_row:, :]
        )
        send(
            level.at[ch, pl.ds(8, ROWS_LOW + REACH - 8), :],
            out_ref.at[0, 0, ch, pl.ds(top_row + 8, ROWS_LOW + REACH - 8), :],
            level_sems.at[ch],
        )
    for copy in copies:
        copy.wait()


def around(value, steps):
    return lax.ppermute(value, "harm", [(i, (i + steps) % RING) for i in range(RING)])


def body(state, forcing, depth, wet_mask, nest_index, freq_order):
    me = lax.axis_index("harm")
    tiles = lax.axis_size("tile")
    smem = pl.BlockSpec(memory_space=pltpu.SMEM)
    hbm = pl.BlockSpec(memory_space=pl.ANY)
    main = pl.BlockSpec(memory_space=pltpu.HBM)
    array = jax.ShapeDtypeStruct

    upper = array((16 * UPPER, LANES), F32)
    parts = pl.pallas_call(
        pack_upper,
        name="pack_upper",
        in_specs=[hbm],
        out_specs=vmem(RING),
        out_shape=(upper,) * RING,
        scratch_shapes=[pltpu.SemaphoreType.DMA((RING, 2))],
        compiler_params=params(),
        cost_estimate=cost(2),
    )(lax.slice(state, (0, 1, 0, 0, 0), (1, 3, 4, ROWS_UP, CELLS)))
    raw = [parts[0]] + [around(parts[slot], slot) for slot in (1, 2, 3)]

    strip, forward, backward = pl.pallas_call(
        prepare,
        name="prepare",
        in_specs=[smem] + vmem(2),
        out_specs=vmem(3),
        out_shape=(array((12, CELLS), F32), array((128, 96), BF16), array((64, 256), BF16)),
        compiler_params=params(),
        cost_estimate=cost(4),
    )(freq_order, nest_index.reshape(1, CELLS), state.reshape(12, CELLS, CELLS))
    strip = lax.ppermute(strip, "sec", [(0, 1)])

    edge_eta = array((4, CELLS), F32)
    packed = pl.pallas_call(
        pack_lower,
        name="pack_lower",
        in_specs=vmem(1) + [hbm],
        out_specs=vmem(RING + 2),
        out_shape=(array((16 * LOWER + 48, LANES), F32),) * RING + (edge_eta, edge_eta),
        scratch_shapes=[
            pltpu.VMEM((2, 3, 4, 8, CELLS), F32),
            pltpu.SemaphoreType.DMA((RING, 2)),
            pltpu.SemaphoreType.DMA((2,)),
        ],
        compiler_params=params(),
        cost_estimate=cost(2),
    )(strip, state)
    first, last = packed[RING:]
    raw_lower = [packed[0]] + [around(packed[slot], slot) for slot in (1, 2, 3)]
    to_next = [(i, i + 1) for i in range(tiles - 1)]
    to_last = [(i + 1, i) for i in range(tiles - 1)]
    made = pl.pallas_call(
        friction_upper,
        name="friction_upper",
        in_specs=vmem(4 + RING),
        out_specs=vmem(RING + 2),
        out_shape=(upper,) * RING + (edge_eta, edge_eta),
        compiler_params=params(),
        cost_estimate=cost(4),
    )(forward, backward, first, last, *raw)
    after = lax.ppermute(made[RING], "tile", to_last)
    before = lax.ppermute(made[RING + 1], "tile", to_next)
    drags = [made[0]] + [around(made[slot], -slot) for slot in (1, 2, 3)]
    plane = array((4, CELLS, CELLS), F32)
    east, north, eta, edge = pl.pallas_call(
        known,
        name="known",
        in_specs=[smem, hbm] + vmem(3),
        out_specs=vmem(4),
        out_shape=(plane, plane, plane, array((8, CELLS), F32)),
        compiler_params=params(),
        cost_estimate=cost(5),
    )(freq_order, made[0], strip, state, forcing)

    made = pl.pallas_call(
        friction_lower,
        name="friction_lower",
        in_specs=vmem(2) + [hbm] + vmem(RING),
        out_specs=vmem(RING + 1),
        out_shape=(array((16 * LOWER, LANES), F32),) * RING + (array((24, CELLS), F32),),
        compiler_params=params(),
        cost_estimate=cost(4),
    )(forward, backward, edge, *raw_lower)
    extra = made[RING]
    drags_lower = [made[0]] + [around(made[slot], -slot) for slot in (1, 2, 3)]

    first, last, edge = pl.pallas_call(
        edge_flux,
        name="edge_flux",
        in_specs=vmem(6),
        out_specs=vmem(3),
        out_shape=(edge_eta, edge_eta, array((8, CELLS), F32)),
        compiler_params=params(),
        cost_estimate=cost(1),
    )(edge, before, after, extra, depth, wet_mask)
    after_flux = lax.ppermute(first, "tile", to_last)
    before_flux = lax.ppermute(last, "tile", to_next)

    whole = array((1, 3, 4, CELLS, CELLS), F32)
    begun, carry = pl.pallas_call(
        finish_upper,
        name="finish_upper",
        in_specs=vmem(6 + RING),
        out_specs=[hbm, vmem(1)[0]],
        out_shape=(whole, array((2, 4, 2 * REACH, CELLS), F32)),
        scratch_shapes=[
            pltpu.VMEM((3, 4, ROWS_UP, CELLS), F32),
            pltpu.VMEM((CELLS, 8), F32),
            pltpu.SemaphoreType.DMA((3,)),
        ],
        compiler_params=params(),
        cost_estimate=cost(3),
    )(extra, depth, wet_mask, east, north, eta, *drags)
    return pl.pallas_call(
        finish_lower,
        name="finish_lower",
        in_specs=vmem(10) + [hbm] + vmem(RING),
        out_specs=hbm,
        out_shape=whole,
        input_output_aliases={10: 0},
        scratch_shapes=[
            pltpu.VMEM((2, 4, REACH + ROWS_LOW, CELLS), F32),
            pltpu.VMEM((4, REACH + ROWS_LOW, CELLS), F32),
            pltpu.VMEM((2, 4, 8, CELLS), F32),
            pltpu.VMEM((CELLS, 8), F32),
            pltpu.SemaphoreType.DMA((4,)),
            pltpu.SemaphoreType.DMA((4,)),
        ],
        compiler_params=params(),
        cost_estimate=cost(3),
    )(extra, edge, before_flux, after_flux, depth, wet_mask, east, north, eta, carry, begun, *drags_lower)


def solution(mesh):
    in_specs = (
        P("sec", None, "harm", "tile", None),
        P("sec", None, "harm", "tile", None),
        P("sec", "tile", None),
        P("sec", "tile", None),
        P("tile"),
        P(),
    )
    out_specs = P("sec", None, "harm", "tile", None)
    return jax.shard_map(body, mesh=mesh, in_specs=in_specs, out_specs=out_specs, check_vma=False)
```

```python
import functools

import jax
import jax.numpy as jnp
from jax import lax
from jax.experimental import pallas as pl
from jax.experimental.pallas import tpu as pltpu
from jax.sharding import PartitionSpec as P

K = 8
NT = 64
CELLS = 256
RING = 4
LANES = 128
UPPER = 32
LOWER = 32
ROWS_UP = RING * UPPER
ROWS_LOW = RING * LOWER
REACH = 16
relax_step = 0.3
speed_floor = 0.01
omega_step = 0.1
TURN = 6.283185307179586 / NT
F32 = jnp.float32
BF16 = jnp.bfloat16
I32 = jnp.int32
MIB = 1 << 20


def params(mib=48):
    return pltpu.CompilerParams(vmem_limit_bytes=mib * MIB)


def cost(us):
    return pl.CostEstimate(flops=0, bytes_accessed=int(us * 3.0e6), transcendentals=0)


def vmem(count):
    return [pl.BlockSpec(memory_space=pltpu.VMEM)] * count


def dot(a, b):
    return jnp.dot(a, b, preferred_element_type=F32)


def pair(x):
    high = x.astype(BF16)
    return high, (x - high.astype(F32)).astype(BF16)


def iota(shape, dim):
    return lax.broadcasted_iota(I32, shape, dim)


def trig(freq_ref, me, time, slot, channel):
    owner = (me - slot + RING) & (RING - 1)
    constituent = owner * 2 + (channel >> 1)
    cycles = jnp.zeros(time.shape, I32)
    for k in range(K):
        cycles = jnp.where(constituent == k, freq_ref[k] + 1, cycles)
    angle = ((time * cycles) & (NT - 1)).astype(F32) * TURN
    return jnp.where((channel & 1) == 0, jnp.cos(angle), jnp.sin(angle))


def prepare(freq_ref, index_ref, fields_ref, strip_ref, forward_ref, backward_ref):
    me = lax.axis_index("harm")
    index = index_ref[...]
    row_of, col_of = index >> 8, index & (CELLS - 1)
    pick = jnp.where(iota((CELLS, CELLS), 0) == col_of, 1.0, 0.0).astype(BF16)
    picks = jnp.concatenate([pick, pick, pick], 0)
    at_row = iota((CELLS, CELLS), 0) == row_of
    for k in range(12):
        plane = fields_ref[k]
        high, rest = plane.astype(BF16), None
        rest = plane - high.astype(F32)
        mid, low = pair(rest)
        column = dot(jnp.concatenate([high, mid, low], 1), picks)
        strip_ref[k : k + 1, :] = jnp.sum(jnp.where(at_row, column, 0.0), axis=0, keepdims=True)
    shape = (128, 96)
    row, col = iota(shape, 0), iota(shape, 1)
    part, lane = col >> 5, col & 31
    value = trig(freq_ref, me, row & 63, lane >> 3, lane & 3)
    value = jnp.where((row >> 6) == ((lane >> 2) & 1), value, 0.0)
    high = value.astype(BF16).astype(F32)
    forward_ref[...] = jnp.where(part == 1, value - high, high).astype(BF16)
    shape = (64, 256)
    row, col = iota(shape, 0), iota(shape, 1)
    lane = row & 31
    value = trig(freq_ref, me, col & 63, lane >> 3, lane & 3) * (1.0 / NT)
    value = jnp.where(((col >> 6) & 1) == ((lane >> 2) & 1), value, 0.0)
    high = value.astype(BF16).astype(F32)
    low = jnp.where(col < 128, value - high, 0.0)
    backward_ref[...] = jnp.where(row < 32, high, low).astype(BF16)


def piece(state_ref, field, out_ref, sem, row, size, j):
    return pltpu.make_async_copy(
        state_ref.at[0, pl.ds(field, 2), :, pl.ds(row, size), pl.ds(j * LANES, LANES)],
        out_ref.reshape(2, 4, size, LANES),
        sem,
    )


def pack_upper(state_ref, *refs):
    outs, sems = refs[:RING], refs[RING]
    me = lax.axis_index("harm")
    copies = []
    for slot in (1, 3, 2, 0):
        row = pl.multiple_of(((me + slot) & (RING - 1)) * UPPER, UPPER)
        for j in range(2):
            out_ref = outs[slot].at[pl.ds(8 * UPPER * j, 8 * UPPER), :]
            copies.append(piece(state_ref, 0, out_ref, sems.at[slot, j], row, UPPER, j))
    for copy in copies:
        copy.start()
    for copy in copies:
        copy.wait()


def pack_lower(strip_ref, state_ref, *refs):
    outs, (first_ref, last_ref, edges, sems, edge_sems) = refs[:RING], refs[RING:]
    me = lax.axis_index("harm")
    shelf = lax.axis_index("sec") == 1
    copies = []
    for e, row in enumerate((0, CELLS - 8)):
        copies.append(
            pltpu.make_async_copy(state_ref.at[0, :, :, pl.ds(row, 8), :], edges.at[e], edge_sems.at[e])
        )
    for slot in range(RING):
        row = pl.multiple_of(ROWS_UP + ((me + slot) & (RING - 1)) * LOWER, 8)
        for j in range(2):
            out_ref = outs[slot].at[pl.ds(8 * LOWER * j, 8 * LOWER), :]
            copies.append(piece(state_ref, 1, out_ref, sems.at[slot, j], row, LOWER, j))
    for copy in copies:
        copy.start()
    for copy in copies[:2]:
        copy.wait()
    strip = strip_ref[...]
    take = jnp.logical_and(iota((12, CELLS), 1) == 0, shelf)
    first = edges[0].reshape(12, 8, CELLS)[:, 0, :]
    last = edges[1].reshape(12, 8, CELLS)[:, 7, :]
    first = jnp.where(take, strip[:, 0:1], first)
    last = jnp.where(take, strip[:, CELLS - 1 : CELLS], last)
    first_ref[...] = first[0:4]
    last_ref[...] = last[0:4]
    for e, values in enumerate((strip, first, last)):
        for j in range(2):
            row = 16 * LOWER + 24 * j + 8 * e
            for out_ref in outs:
                out_ref[row : row + 8, :] = values[4:12, j * LANES : (j + 1) * LANES]
    for copy in copies[2:]:
        copy.wait()


def terms(forward, backward, x):
    high, low = pair(x)
    samples = dot(forward, jnp.concatenate([high, high, low], 0))
    east, north = samples[:NT], samples[NT:]
    square = east * east + north * north + speed_floor
    speed = square * lax.rsqrt(square)
    high, low = pair(jnp.concatenate([speed * east, speed * north], 0))
    both = dot(backward, jnp.concatenate([high, low], 0))
    return both[:32] + both[32:]


def rows_terms(size, forward, backward, xs, outs):
    def step(r, carry):
        rows = [pl.ds(8 * size * j + r, 8, stride=size) for j in range(2)]
        halves = [jnp.concatenate([ref[rows[j], :] for ref in xs], 0) for j in range(2)]
        out = terms(forward, backward, jnp.concatenate(halves, 1))
        for slot in range(RING):
            for j in range(2):
                outs[slot][rows[j], :] = out[8 * slot : 8 * slot + 8, j * LANES : (j + 1) * LANES]
        return carry

    lax.fori_loop(0, size, step, 0, unroll=16)


def friction_upper(forward_ref, backward_ref, first_ref, last_ref, *refs):
    rows_terms(UPPER, forward_ref[...], backward_ref[...], refs[:RING], refs[RING : 2 * RING])
    refs[2 * RING][...] = first_ref[...]
    refs[2 * RING + 1][...] = last_ref[...]


def friction_lower(forward_ref, backward_ref, behind_ref, *refs):
    xs, outs, extra_ref = refs[:RING], refs[RING : 2 * RING], refs[2 * RING]
    forward, backward = forward_ref[...], backward_ref[...]
    rows_terms(LOWER, forward, backward, xs, outs)
    for e in range(3):
        rows = [pl.ds(16 * LOWER + 24 * j + 8 * e, 8) for j in range(2)]
        halves = [jnp.concatenate([ref[rows[j], :] for ref in xs], 0) for j in range(2)]
        extra_ref[8 * e : 8 * e + 8, :] = terms(forward, backward, jnp.concatenate(halves, 1))[:8]


def left_right(x):
    lane = iota(x.shape, 1)
    right = jnp.where(lane == CELLS - 1, 0.0, pltpu.roll(x, CELLS - 1, 1))
    left = jnp.where(lane == 0, 0.0, pltpu.roll(x, 1, 1))
    return right - left


def up_down(x, before, after):
    count = x.shape[0]
    row = iota(x.shape, 0)
    down = jnp.where(row == count - 1, after, pltpu.roll(x, count - 1, 0))
    up = jnp.where(row == 0, before, pltpu.roll(x, 1, 0))
    return down - up


def known(freq_ref, behind_ref, strip_ref, state_ref, forcing_ref, east_ref, north_ref, eta_ref, edge_ref):
    me = lax.axis_index("harm")
    shelf = lax.axis_index("sec") == 1
    take = jnp.logical_and(iota((CELLS, LANES), 1) == 0, shelf)
    columns = jnp.concatenate([strip_ref[...], jnp.zeros((4, CELLS), F32)], 0).T

    def field(f, ch):
        k = 4 * f + ch
        left = jnp.where(take, columns[:, k : k + 1], state_ref[0, f, ch, :, :LANES])
        return jnp.concatenate([left, state_ref[0, f, ch, :, LANES:]], 1)

    for i in range(2):
        omega = omega_step * (freq_ref[2 * me + i] + 1).astype(F32)
        eta = [field(0, 2 * i + p) for p in range(2)]
        for p in range(2):
            ch = 2 * i + p
            turn = -omega if p else omega
            eta_ref[ch] = eta[p] - relax_step * (turn * eta[1 - p])
        east = [field(1, 2 * i + p) for p in range(2)]
        for p in range(2):
            ch = 2 * i + p
            turn = -omega if p else omega
            rest = turn * east[1 - p] + 0.5 * left_right(eta[p]) - forcing_ref[0, 0, ch]
            east_ref[ch] = east[p] - relax_step * rest
        north = [field(2, 2 * i + p) for p in range(2)]
        for p in range(2):
            ch = 2 * i + p
            turn = -omega if p else omega
            slope = up_down(eta[p], 0.0, 0.0)
            rest = turn * north[1 - p] + 0.5 * slope - forcing_ref[0, 1, ch]
            value = north[p] - relax_step * rest
            north_ref[ch] = value
            edge_ref[ch : ch + 1, :] = value[0:1, :]
            edge_ref[4 + ch : 5 + ch, :] = value[CELLS - 1 : CELLS, :]


def edge_flux(edge_ref, before_ref, after_ref, extra_ref, depth_ref, wet_ref, first_ref, last_ref, north_ref):
    half = 0.5 * relax_step
    for out_ref, at, row, beside in (
        (first_ref, 0, 0, half * before_ref[...]),
        (last_ref, 1, CELLS - 1, -half * after_ref[...]),
    ):
        height = depth_ref[0, row : row + 1, :]
        wet = wet_ref[0, row : row + 1, :].astype(F32)
        drag = extra_ref[8 + 8 * at + 4 : 8 + 8 * at + 8, :]
        north = wet * (edge_ref[4 * at : 4 * at + 4, :] + beside - (relax_step / height) * drag)
        out_ref[...] = height * north
        north_ref[4 * at : 4 * at + 4, :] = north


def transports(start, size, turned, extra_ref, depth_ref, wet_ref, sources, drags, store):
    me = lax.axis_index("harm")
    shelf = lax.axis_index("sec") == 1
    take = jnp.logical_and(iota((size, LANES), 1) == 0, shelf)
    turned[...] = extra_ref[0:8, :].T
    for slot in range(RING):
        at = pl.multiple_of(((me + slot) & (RING - 1)) * size, 8)
        rows = pl.ds(start + at, size)
        columns = turned[rows, :]
        wet = wet_ref[0, rows, :].astype(F32)
        factor = relax_step / depth_ref[0, rows, :]
        for k in range(8):
            left, right = (
                drags[slot][pl.ds((8 * j + k) * size, size), :] for j in range(2)
            )
            left = jnp.where(take, columns[:, k : k + 1], left)
            drag = jnp.concatenate([left, right], 1)
            store(1 + k // 4, k % 4, at, wet * (sources[k // 4][k % 4, rows, :] - factor * drag))


def new_eta(east, north, before, after, height, wet, eta):
    slope = left_right(height * east) + up_down(height * north, before, after)
    return wet * (eta - (0.5 * relax_step) * slope)


def finish_upper(extra_ref, depth_ref, wet_ref, east_ref, north_ref, eta_ref, *refs):
    slots, (out_ref, carry_ref, made, turned, sems) = refs[:RING], refs[RING:]

    def store(f, ch, row, value):
        made[f, ch, pl.ds(row, UPPER), :] = value

    transports(0, UPPER, turned, extra_ref, depth_ref, wet_ref, (east_ref, north_ref), slots, store)
    copies = []
    for f in (1, 2, 0):
        if f == 0:
            height = depth_ref[0, :ROWS_UP, :]
            wet = wet_ref[0, :ROWS_UP, :].astype(F32)
            for ch in range(4):
                made[0, ch] = new_eta(made[1, ch], made[2, ch], 0.0, 0.0, height, wet, eta_ref[ch, :ROWS_UP, :])
        copy = pltpu.make_async_copy(made.at[f], out_ref.at[0, f, :, pl.ds(0, ROWS_UP), :], sems.at[f])
        copy.start()
        copies.append(copy)
    for f in range(2):
        for ch in range(4):
            carry_ref[f, ch, :REACH, :] = made[1 + f, ch, :REACH, :]
            carry_ref[f, ch, REACH:, :] = made[1 + f, ch, ROWS_UP - REACH :, :]
    for copy in copies:
        copy.wait()


def finish_lower(
    extra_ref, edge_ref, before_ref, after_ref, depth_ref, wet_ref, east_ref, north_ref, eta_ref, carry_ref, begun_ref, *refs
):
    slots, (out_ref, made, level, top, turned, sems, level_sems) = refs[:RING], refs[RING:]
    top_row = ROWS_UP - REACH
    for f in range(2):
        for ch in range(4):
            made[f, ch, :REACH, :] = carry_ref[f, ch, REACH:, :]

    def store(f, ch, row, value):
        made[f - 1, ch, pl.ds(REACH + row, LOWER), :] = value

    transports(ROWS_UP, LOWER, turned, extra_ref, depth_ref, wet_ref, (east_ref, north_ref), slots, store)
    for ch in range(4):
        made[1, ch, REACH + ROWS_LOW - 1 : REACH + ROWS_LOW, :] = edge_ref[4 + ch : 5 + ch, :]
    copies = []

    def send(source, target, sem):
        copy = pltpu.make_async_copy(source, target, sem)
        copy.start()
        copies.append(copy)

    for f in range(2):
        send(
            made.at[f, :, pl.ds(REACH, ROWS_LOW), :],
            out_ref.at[0, 1 + f, :, pl.ds(ROWS_UP, ROWS_LOW), :],
            sems.at[f],
        )
    height = depth_ref[0, :REACH, :]
    wet = wet_ref[0, :REACH, :].astype(F32)
    for ch in range(4):
        north = carry_ref[1, ch, :REACH, :]
        north = jnp.where(iota((REACH, CELLS), 0) == 0, edge_ref[ch : ch + 1, :], north)
        value = new_eta(
            carry_ref[0, ch, :REACH, :], north, before_ref[ch : ch + 1, :], 0.0, height, wet, eta_ref[ch, :REACH, :]
        )
        top[0, ch] = value[:8]
        top[1, ch] = north[:8]
    for i in range(2):
        send(top.at[i], out_ref.at[0, 2 * i, :, pl.ds(0, 8), :], sems.at[2 + i])
    height = depth_ref[0, top_row:, :]
    wet = wet_ref[0, top_row:, :].astype(F32)
    for ch in range(4):
        level[ch] = new_eta(
            made[0, ch], made[1, ch], 0.0, after_ref[ch : ch + 1, :], height, wet, eta_ref[ch, top_row:, :]
        )
        send(
            level.at[ch, pl.ds(8, ROWS_LOW + REACH - 8), :],
            out_ref.at[0, 0, ch, pl.ds(top_row + 8, ROWS_LOW + REACH - 8), :],
            level_sems.at[ch],
        )
    for copy in copies:
        copy.wait()


def around(value, steps):
    return lax.ppermute(value, "harm", [(i, (i + steps) % RING) for i in range(RING)])


def body(state, forcing, depth, wet_mask, nest_index, freq_order):
    me = lax.axis_index("harm")
    tiles = lax.axis_size("tile")
    smem = pl.BlockSpec(memory_space=pltpu.SMEM)
    hbm = pl.BlockSpec(memory_space=pl.ANY)
    main = pl.BlockSpec(memory_space=pltpu.HBM)
    array = jax.ShapeDtypeStruct

    upper = array((16 * UPPER, LANES), F32)
    parts = pl.pallas_call(
        pack_upper,
        name="pack_upper",
        in_specs=[hbm],
        out_specs=vmem(RING),
        out_shape=(upper,) * RING,
        scratch_shapes=[pltpu.SemaphoreType.DMA((RING, 2))],
        compiler_params=params(),
        cost_estimate=cost(2),
    )(lax.slice(state, (0, 1, 0, 0, 0), (1, 3, 4, ROWS_UP, CELLS)))
    raw = [parts[0]] + [around(parts[slot], slot) for slot in (1, 2, 3)]

    strip, forward, backward = pl.pallas_call(
        prepare,
        name="prepare",
        in_specs=[smem] + vmem(2),
        out_specs=vmem(3),
        out_shape=(array((12, CELLS), F32), array((128, 96), BF16), array((64, 256), BF16)),
        compiler_params=params(),
        cost_estimate=cost(4),
    )(freq_order, nest_index.reshape(1, CELLS), state.reshape(12, CELLS, CELLS))
    strip = lax.ppermute(strip, "sec", [(0, 1)])

    edge_eta = array((4, CELLS), F32)
    packed = pl.pallas_call(
        pack_lower,
        name="pack_lower",
        in_specs=vmem(1) + [hbm],
        out_specs=vmem(RING + 2),
        out_shape=(array((16 * LOWER + 48, LANES), F32),) * RING + (edge_eta, edge_eta),
        scratch_shapes=[
            pltpu.VMEM((2, 3, 4, 8, CELLS), F32),
            pltpu.SemaphoreType.DMA((RING, 2)),
            pltpu.SemaphoreType.DMA((2,)),
        ],
        compiler_params=params(),
        cost_estimate=cost(2),
    )(strip, state)
    first, last = packed[RING:]
    raw_lower = [packed[0]] + [around(packed[slot], slot) for slot in (1, 2, 3)]
    to_next = [(i, i + 1) for i in range(tiles - 1)]
    to_last = [(i + 1, i) for i in range(tiles - 1)]
    made = pl.pallas_call(
        friction_upper,
        name="friction_upper",
        in_specs=vmem(4 + RING),
        out_specs=vmem(RING + 2),
        out_shape=(upper,) * RING + (edge_eta, edge_eta),
        compiler_params=params(),
        cost_estimate=cost(4),
    )(forward, backward, first, last, *raw)
    after = lax.ppermute(made[RING], "tile", to_last)
    before = lax.ppermute(made[RING + 1], "tile", to_next)
    drags = [made[0]] + [around(made[slot], -slot) for slot in (1, 2, 3)]
    plane = array((4, CELLS, CELLS), F32)
    east, north, eta, edge = pl.pallas_call(
        known,
        name="known",
        in_specs=[smem, hbm] + vmem(3),
        out_specs=vmem(4),
        out_shape=(plane, plane, plane, array((8, CELLS), F32)),
        compiler_params=params(),
        cost_estimate=cost(5),
    )(freq_order, made[0], strip, state, forcing)

    made = pl.pallas_call(
        friction_lower,
        name="friction_lower",
        in_specs=vmem(2) + [hbm] + vmem(RING),
        out_specs=vmem(RING + 1),
        out_shape=(array((16 * LOWER, LANES), F32),) * RING + (array((24, CELLS), F32),),
        compiler_params=params(),
        cost_estimate=cost(4),
    )(forward, backward, edge, *raw_lower)
    extra = made[RING]
    drags_lower = [made[0]] + [around(made[slot], -slot) for slot in (1, 2, 3)]

    first, last, edge = pl.pallas_call(
        edge_flux,
        name="edge_flux",
        in_specs=vmem(6),
        out_specs=vmem(3),
        out_shape=(edge_eta, edge_eta, array((8, CELLS), F32)),
        compiler_params=params(),
        cost_estimate=cost(1),
    )(edge, before, after, extra, depth, wet_mask)
    after_flux = lax.ppermute(first, "tile", to_last)
    before_flux = lax.ppermute(last, "tile", to_next)

    whole = array((1, 3, 4, CELLS, CELLS), F32)
    begun, carry = pl.pallas_call(
        finish_upper,
        name="finish_upper",
        in_specs=vmem(6 + RING),
        out_specs=[hbm, vmem(1)[0]],
        out_shape=(whole, array((2, 4, 2 * REACH, CELLS), F32)),
        scratch_shapes=[
            pltpu.VMEM((3, 4, ROWS_UP, CELLS), F32),
            pltpu.VMEM((CELLS, 8), F32),
            pltpu.SemaphoreType.DMA((3,)),
        ],
        compiler_params=params(),
        cost_estimate=cost(3),
    )(extra, depth, wet_mask, east, north, eta, *drags)
    return pl.pallas_call(
        finish_lower,
        name="finish_lower",
        in_specs=vmem(10) + [hbm] + vmem(RING),
        out_specs=hbm,
        out_shape=whole,
        input_output_aliases={10: 0},
        scratch_shapes=[
            pltpu.VMEM((2, 4, REACH + ROWS_LOW, CELLS), F32),
            pltpu.VMEM((4, REACH + ROWS_LOW, CELLS), F32),
            pltpu.VMEM((2, 4, 8, CELLS), F32),
            pltpu.VMEM((CELLS, 8), F32),
            pltpu.SemaphoreType.DMA((4,)),
            pltpu.SemaphoreType.DMA((4,)),
        ],
        compiler_params=params(),
        cost_estimate=cost(3),
    )(extra, edge, before_flux, after_flux, depth, wet_mask, east, north, eta, carry, begun, *drags_lower)


def solution(mesh):
    in_specs = (
        P("sec", None, "harm", "tile", None),
        P("sec", None, "harm", "tile", None),
        P("sec", "tile", None),
        P("sec", "tile", None),
        P("tile"),
        P(),
    )
    out_specs = P("sec", None, "harm", "tile", None)
    return jax.shard_map(body, mesh=mesh, in_specs=in_specs, out_specs=out_specs, check_vma=False)
```
